256 devices in a mesh: row: 16 (over x, z_hi), col: 16 (over z_lo, y, core).
Axes of the slice: x: 4, y: 4, z: 8 (z_hi: 4, z_lo: 2; z = z_hi * 2 + z_lo), core: 2. Of those that a mesh axis runs over, the one named last changes fastest.
Arguments:
- pair: bfloat16 [512, 512, 128], P('row', 'col'), may hold values from -6 to 6
- pair_mask: int32 [512, 512], P('row', 'col'), may hold values 0 or 1
- norm_in_gain: float32 [2, 128], replicated, may hold values from 0.5 to 1.5
- norm_in_bias: float32 [2, 128], replicated, may hold values from -3 to 3
- proj_weight: bfloat16 [2, 128, 256], replicated, may hold values from -0.5 to 0.5
- proj_gate: bfloat16 [2, 128, 256], replicated, may hold values from -0.5 to 0.5
- out_gate: bfloat16 [2, 128, 128], replicated, may hold values from -0.5 to 0.5
- norm_out_gain: float32 [2, 128], replicated, may hold values from 0.5 to 1.5
- norm_out_bias: float32 [2, 128], replicated, may hold values from -3 to 3
- out_weight: bfloat16 [2, 128, 128], replicated, may hold values from -0.5 to 0.5
Outputs:
- updated: bfloat16 [512, 512, 128], P('row', 'col')
The draws below stay inside these ranges and needn't reach their ends.
All inputs are finite; a program needn't handle non-finite values. No bound on the sum of `pair_mask` on one device may be relied on, other than what follows from the above.
Results may differ from the reference program's by a relative error of at most 0.015.
Values may be sent and summed in bfloat16 or wider, within the bound.
No kernel may reach another device: no remote copies, remote signals or barrier semaphores. Data moves between devices by JAX's collectives and lax.ppermute only.
A program may use at most 128 MiB of HBM per device.

```python
import jax
import jax.numpy as jnp
from jax import lax

C = 128
TOKENS = 512


def touch_ends(entries, own_key, least, largest):
    place = [jax.random.randint(jax.random.fold_in(own_key, axis), (), 0, length) for axis, length in enumerate(entries.shape)]
    widest = entries.shape.index(max(entries.shape))
    neighbour = place[:widest] + [(place[widest] + 1) % entries.shape[widest]] + place[widest + 1:]
    return entries.at[tuple(place)].set(least).at[tuple(neighbour)].set(largest)


def block_levels(key, dims, shards, low, high):
    loudness = 1.0
    for dim, shards_of in shards:
        heights = jax.random.uniform(jax.random.fold_in(jax.random.fold_in(key, 6), dim), (shards_of,), jnp.float32, low / len(shards), high / len(shards))
        loudness = loudness * jnp.repeat(jnp.exp(heights), dims[dim] // shards_of).reshape((-1,) + (1,) * (len(dims) - 1 - dim))
    return loudness


def normal_values(own_key, shape, deviation, bound, pieces=(), kind=jnp.bfloat16):
    drawn = jax.random.normal(own_key, shape, jnp.float32) * deviation
    if len(pieces) > 0:
        drawn = block_levels(own_key, shape, pieces, -0.22, 0.18) * drawn
    return jnp.clip(drawn, min=-bound, max=bound).astype(kind)


def setup_inputs(seed: int = 0) -> dict:
    arg_keys = jax.random.split(jax.random.key(seed), 11)
    pair = normal_values(arg_keys[0], (TOKENS, TOKENS, C), 1.0, 6.0, ((0, 16), (1, 16)))
    pair_mask = touch_ends((jax.random.randint(arg_keys[1], (TOKENS, TOKENS), 0, 8) < 7).astype(jnp.int32), jax.random.fold_in(arg_keys[1], 1), 0, 1)
    norm_in_gain = jnp.clip(1.0 + 0.1 * jax.random.normal(arg_keys[2], (2, C), jnp.float32), 0.5, 1.5)
    norm_in_bias = normal_values(arg_keys[3], (2, C), 0.5, 3.0, (), jnp.float32)
    proj_weight = normal_values(arg_keys[4], (2, C, 2 * C), C ** -0.5, 0.5)
    proj_gate = normal_values(arg_keys[5], (2, C, 2 * C), C ** -0.5, 0.5)
    out_gate = normal_values(arg_keys[6], (2, C, C), C ** -0.5, 0.5)
    norm_out_gain = jnp.clip(1.0 + 0.1 * jax.random.normal(arg_keys[7], (2, C), jnp.float32), 0.5, 1.5)
    norm_out_bias = normal_values(arg_keys[8], (2, C), 0.5, 3.0, (), jnp.float32)
    out_weight = normal_values(arg_keys[9], (2, C, C), C ** -0.5, 0.5)
    return dict(pair=pair, pair_mask=pair_mask, norm_in_gain=norm_in_gain, norm_in_bias=norm_in_bias, proj_weight=proj_weight, proj_gate=proj_gate, out_gate=out_gate, norm_out_gain=norm_out_gain, norm_out_bias=norm_out_bias, out_weight=out_weight)


def layer_norm(values, gain_vec, bias_vec):
    average = lax.optimization_barrier(jnp.mean(values, axis=-1, keepdims=True))
    centered = values - average
    variance = lax.optimization_barrier(jnp.mean(centered * centered, axis=-1, keepdims=True))
    return centered * lax.rsqrt(variance + 1e-05) * gain_vec + bias_vec

def triangle(pair, mask_float, layer_index, outgoing, params):
    norm_in_gain, norm_in_bias, proj_weight, proj_gate, out_gate, norm_out_gain, norm_out_bias, out_weight = params
    pair_float = pair.astype(jnp.float32)
    normed = layer_norm(pair_float, norm_in_gain[layer_index], norm_in_bias[layer_index]).astype(jnp.bfloat16)
    projected = jnp.dot(normed, proj_weight[layer_index], preferred_element_type=jnp.float32)
    gate_proj = jnp.dot(normed, proj_gate[layer_index], preferred_element_type=jnp.float32)
    operands = (jax.nn.sigmoid(gate_proj) * projected * mask_float).astype(jnp.bfloat16)
    left_side = operands[..., :C].astype(jnp.float32)
    right_side = operands[..., C:].astype(jnp.float32)
    if outgoing:
        product = jnp.einsum('ikc,jkc->ijc', left_side, right_side)
    else:
        product = jnp.einsum('kic,kjc->ijc', left_side, right_side)
    product_normed = layer_norm(product, norm_out_gain[layer_index], norm_out_bias[layer_index]).astype(jnp.bfloat16)
    out_gated = jax.nn.sigmoid(jnp.dot(normed, out_gate[layer_index], preferred_element_type=jnp.float32))
    update = out_gated * jnp.dot(product_normed, out_weight[layer_index], preferred_element_type=jnp.float32)
    return (pair_float + update).astype(jnp.bfloat16)

def reference(pair, pair_mask, norm_in_gain, norm_in_bias, proj_weight, proj_gate, out_gate, norm_out_gain, norm_out_bias, out_weight):
    params = (norm_in_gain, norm_in_bias, proj_weight, proj_gate, out_gate, norm_out_gain, norm_out_bias, out_weight)
    mask_float = pair_mask.astype(jnp.float32)[..., None]
    first_pass = triangle(pair, mask_float, 0, True, params)
    return triangle(first_pass, mask_float, 1, False, params)
```

```python
import jax
import jax.numpy as jnp
from jax import lax
from jax.experimental import pallas as pl
from jax.experimental.pallas import tpu as pltpu
from jax.sharding import Mesh
from jax.sharding import PartitionSpec as P

C = 128
T = 32
F32 = jnp.float32
BF16 = jnp.bfloat16
CHIPS = ("x", "zh", "zl", "y")
VMEM_LIMIT = 32 * 1024 * 1024


def dot(a, b):
    return jnp.dot(a, b, preferred_element_type=F32)


def dot_nt(a, b):
    return lax.dot_general(a, b, (((1,), (1,)), ((), ())), preferred_element_type=F32)


def sigmoid(v):
    return 0.5 * jnp.tanh(0.5 * v) + 0.5


def layer_norm_lanes(values, gain, bias):
    average = jnp.mean(values, axis=-1, keepdims=True)
    centered = values - average
    variance = jnp.mean(centered * centered, axis=-1, keepdims=True)
    return centered * lax.rsqrt(variance + 1e-05) * gain + bias


def iota(shape, dim):
    return lax.broadcasted_iota(jnp.int32, shape, dim)


def group_select(rows):
    group = iota((8, C), 1) // T
    out = rows[0:8]
    for q in range(1, 4):
        out = jnp.where(group == q, rows[8 * q : 8 * q + 8], out)
    return out


def swap_groups():
    src = iota((4 * C, 4 * C), 0)
    dst = iota((4 * C, 4 * C), 1)
    back = (dst & (T - 1)) | (((dst >> 5) & 3) << 7) | ((dst >> 7) << 5)
    return jnp.where(src == back, 1.0, 0.0).astype(BF16)


def emit_operands(normed, mask_row, weight_t, gate_t, scratch, s):
    projected = dot_nt(weight_t, normed)
    gate = dot_nt(gate_t, normed)
    operands = sigmoid(gate) * projected * mask_row
    scratch[pl.ds(s, C, stride=16), :] = operands[:C]
    scratch[pl.ds(8 + s, C, stride=16), :] = operands[C:]


def first_kernel(pair, mask, gain, bias, weight, gate, out_gate, lr, g_out, scratch):
    weight_t = weight[0].T
    gate_t = gate[0].T
    wide = jnp.where((iota((T, C), 1) & (T - 1)) == iota((T, C), 0), 1.0, 0.0).astype(BF16)
    mask_rows = group_select(dot(mask[...].astype(F32).astype(BF16), wide))
    for s in range(8):
        x = jnp.concatenate([pair[8 * q + s].astype(F32) for q in range(4)], axis=0)
        normed = layer_norm_lanes(x, gain[0:1, :], bias[0:1, :]).astype(BF16)
        opened = sigmoid(dot(normed, out_gate[0]))
        for q in range(4):
            g_out[pl.ds((8 * q + s) * T, T), :] = opened[q * T : (q + 1) * T]
        emit_operands(normed, mask_rows[s : s + 1], weight_t, gate_t, scratch, s)
    lr[...] = scratch[...].reshape(C, 16, C).astype(BF16)


def product_normed_rows(y, gain, bias, scratch, layer):
    values = y[...].astype(F32)
    average = jnp.mean(values, axis=0, keepdims=True)
    centered = values - average
    variance = jnp.mean(centered * centered, axis=0, keepdims=True)
    scratch[...] = (centered * lax.rsqrt(variance + 1e-05)).reshape(8 * C, C)
    gain_full = jnp.broadcast_to(gain[layer : layer + 1, :], (C, C)).T
    bias_full = jnp.broadcast_to(bias[layer : layer + 1, :], (C, C)).T
    return gain_full, bias_full


def update_rows(scratch, s, gain_full, bias_full, weight):
    normed = scratch[pl.ds(s, C, stride=8), :] * gain_full + bias_full
    return dot(normed.T.astype(BF16), weight)


def middle_kernel(
    y, pair, g_in, mask, in_gain, in_bias, weight, gate, out_gate, out_gain, out_bias, out_weight,
    lr, z_out, g_out, scratch, scratch_y, scratch_z,
):
    weight_t = weight[1].T
    gate_t = gate[1].T
    four = jnp.concatenate([mask[...].astype(F32).astype(BF16)] * 4, axis=0)
    eye = jnp.where(iota((T, T), 1) == iota((T, T), 0), 1.0, 0.0).astype(BF16)
    mask_rows = group_select(dot_nt(eye, four))
    scratch_z[...] = pair[...].astype(F32).reshape(T * T, C)
    gain_full, bias_full = product_normed_rows(y, out_gain, out_bias, scratch_y, 0)
    for s in range(8):
        update = update_rows(scratch_y, s, gain_full, bias_full, out_weight[0])
        rows = [pl.ds(8 * q + s, T, stride=T) for q in range(4)]
        z = jnp.concatenate([scratch_z[r, :] for r in rows], axis=0)
        g = jnp.concatenate([g_in[r, :] for r in rows], axis=0)
        z = (z + g * update).astype(BF16).astype(F32)
        normed = layer_norm_lanes(z, in_gain[1:2, :], in_bias[1:2, :]).astype(BF16)
        opened = sigmoid(dot(normed, out_gate[1]))
        for q in range(4):
            z_out[rows[q], :] = z[q * T : (q + 1) * T]
            g_out[rows[q], :] = opened[q * T : (q + 1) * T]
        emit_operands(normed, mask_rows[s : s + 1], weight_t, gate_t, scratch, s)
    lr[...] = scratch[...].reshape(C, 16, C).astype(BF16)


def last_kernel(y, z_in, g_in, out_gain, out_bias, out_weight, out, scratch_y):
    gain_full, bias_full = product_normed_rows(y, out_gain, out_bias, scratch_y, 1)
    for s in range(8):
        update = update_rows(scratch_y, s, gain_full, bias_full, out_weight[1])
        for q in range(4):
            rows = pl.ds((8 * q + s) * T, T)
            piece = z_in[rows, :] + g_in[rows, :] * update[q * T : (q + 1) * T]
            out[8 * q + s] = piece.astype(BF16)


def outgoing_kernel(core, own, other, out, left, right):
    swap = swap_groups()
    half = core[0]
    for part, src in enumerate((own, other)):
        for quad in range(2):
            y = jnp.concatenate(
                [src[:, 4 * quad + c].reshape(256, C) for c in range(4)], axis=1
            )
            z = dot(y, swap).reshape(16, 16, 4 * C)
            depth = pl.ds((2 * part + quad) * C, C)
            for q in range(4):
                left[:, q, :, depth] = z[:, :8, q * C : (q + 1) * C]
                right[:, q, :, depth] = z[:, 8:, q * C : (q + 1) * C]
    a = left[...].reshape(512, 512).astype(BF16)
    pairs = right.reshape(8, 2, 4, 8, 512)
    b = jnp.concatenate([pairs[:, half, q].reshape(64, 512) for q in range(4)], axis=0)
    product = dot_nt(b.astype(BF16), a).astype(BF16)
    for quad in range(4):
        y = jnp.concatenate(
            [product[64 * q : 64 * q + 64, quad * C : (quad + 1) * C] for q in range(4)], axis=1
        )
        z = dot(y, swap)
        for r in range(4):
            out[4 * quad + r] = z[:, r * C : (r + 1) * C].reshape(8, 8, C).astype(BF16)


def incoming_kernel(core, own, other, out, left, right):
    swap = swap_groups()
    half = core[0]
    for part, src in enumerate((own, other)):
        for quad in range(4):
            y = jnp.concatenate([src[4 * quad + r].reshape(C, C) for r in range(4)], axis=1)
            z = dot(y, swap).reshape(8, 16, 4 * C)
            depth = pl.ds(quad * C, C)
            for q in range(4):
                left[q, part, :, :, depth] = z[:, :8, q * C : (q + 1) * C]
                if part == 0:
                    right[:, q, :, depth] = z[:, 8:, q * C : (q + 1) * C]
    a = left[...].reshape(512, 512).astype(BF16)
    b = right[...].reshape(256, 512).astype(BF16)
    product = dot_nt(a, b).astype(BF16)
    for quad in range(2):
        y = jnp.concatenate(
            [product[C * q : C * q + C, quad * C : (quad + 1) * C] for q in range(4)], axis=1
        )
        z = dot(y, swap)
        for c in range(4):
            piece = z[:, c * C : (c + 1) * C].reshape(2, 8, 8, C).astype(BF16)
            out[:, half, 4 * quad + c] = piece[0]
            out[:, 1 - half, 4 * quad + c] = piece[1]


def call(kernel, out_shape, scratch, *args, smem=0):
    vmem = pl.BlockSpec(memory_space=pltpu.VMEM)
    scalars = pl.BlockSpec(memory_space=pltpu.SMEM)
    return pl.pallas_call(
        kernel,
        out_shape=out_shape,
        in_specs=[scalars] * smem + [vmem] * (len(args) - smem),
        out_specs=[vmem] * len(out_shape) if isinstance(out_shape, list) else vmem,
        scratch_shapes=[pltpu.VMEM(shape, F32) for shape in scratch],
        compiler_params=pltpu.CompilerParams(vmem_limit_bytes=VMEM_LIMIT),
    )(*args)


def struct(shape, dtype):
    return jax.ShapeDtypeStruct(shape, dtype)


def exchange(values):
    return lax.all_to_all(values, CHIPS, 0, 0)


def other_core(values):
    return lax.ppermute(values, "core", [(0, 1), (1, 0)])


def on_device(
    pair, pair_mask, in_gain, in_bias, weight, gate, out_gate, out_gain, out_bias, out_weight
):
    core = lax.axis_index("core").astype(jnp.int32).reshape(1)
    operands = struct((C, 16, C), BF16)
    rows = struct((T * T, C), F32)
    lr, g = call(
        first_kernel, [operands, rows], [(16 * C, C)],
        pair, pair_mask, in_gain, in_bias, weight, gate, out_gate,
    )
    own = exchange(lr)
    other = other_core(own)
    y = call(
        outgoing_kernel, struct((16, 8, 8, C), BF16), [(16, 4, 8, 512), (16, 4, 8, 512)],
        core, own.reshape(16, 8, 16, C), other.reshape(16, 8, 16, C), smem=1,
    )
    y = exchange(y.reshape(C, 8, C))
    lr, z, g = call(
        middle_kernel, [operands, rows, rows], [(16 * C, C), (8 * C, C), (T * T, C)],
        y, pair, g, pair_mask, in_gain, in_bias, weight, gate, out_gate, out_gain, out_bias,
        out_weight,
    )
    own = exchange(lr)
    other = other_core(own)
    y = call(
        incoming_kernel, struct((8, 2, 8, 8, C), BF16), [(4, 2, 8, 8, 512), (8, 4, 8, 512)],
        core, own.reshape(16, 8, 16, C), other.reshape(16, 8, 16, C), smem=1,
    )
    y = exchange(y.reshape(C, 8, C))
    return call(
        last_kernel, struct((T, T, C), BF16), [(8 * C, C)],
        y, z, g, out_gain, out_bias, out_weight,
    )


def solution(mesh):
    chips = Mesh(mesh.devices.reshape(4, 4, 2, 4, 2), CHIPS + ("core",))
    tile = P(("x", "zh"), ("zl", "y", "core"))
    return jax.shard_map(
        on_device,
        mesh=chips,
        in_specs=(tile, tile) + (P(),) * 8,
        out_specs=tile,
        check_vma=False,
    )
```

```python
import jax
import jax.numpy as jnp
from jax import lax
from jax.experimental import pallas as pl
from jax.experimental.pallas import tpu as pltpu
from jax.sharding import Mesh
from jax.sharding import PartitionSpec as P

C = 128
T = 32
F32 = jnp.float32
BF16 = jnp.bfloat16
AXES = ("x1", "x0", "zh1", "zh0", "zl", "y1", "y0", "core")
CHIPS = AXES[:-1]
VMEM_LIMIT = 32 * 1024 * 1024


def dot(a, b):
    return jnp.dot(a, b, preferred_element_type=F32)


def dot_nt(a, b):
    return lax.dot_general(a, b, (((1,), (1,)), ((), ())), preferred_element_type=F32)


def sigmoid(v):
    return 0.5 * jnp.tanh(0.5 * v) + 0.5


def normalize(values, axis):
    average = jnp.mean(values, axis=axis, keepdims=True)
    centered = values - average
    variance = jnp.mean(centered * centered, axis=axis, keepdims=True)
    return centered * lax.rsqrt(variance + 1e-05)


def iota(shape, dim):
    return lax.broadcasted_iota(jnp.int32, shape, dim)


def group_select(rows):
    group = iota((8, C), 1) // T
    out = rows[0:8]
    for q in range(1, 4):
        out = jnp.where(group == q, rows[8 * q : 8 * q + 8], out)
    return out


def as_column(vector):
    return jnp.broadcast_to(vector, (C, C)).T


def swap_groups():
    src = iota((4 * C, 4 * C), 0)
    dst = iota((4 * C, 4 * C), 1)
    back = (dst & (T - 1)) | (((dst >> 5) & 3) << 7) | ((dst >> 7) << 5)
    return jnp.where(src == back, 1.0, 0.0).astype(BF16)


def emit_operands(projected, gate, mask_row, scratch, s):
    operands = sigmoid(gate) * projected * mask_row
    scratch[pl.ds(s, C, stride=16), :] = operands[:C]
    scratch[pl.ds(8 + s, C, stride=16), :] = operands[C:]


def first_kernel(
    pair_hbm, mask_hbm, gain_hbm, bias_hbm, weight_hbm, gate_hbm, lr,
    pair, mask, gain, bias, weight, gate, scratch, sems,
):
    moves = [
        (gain_hbm, gain), (bias_hbm, bias), (weight_hbm.at[0], weight), (gate_hbm.at[0], gate),
        (mask_hbm, mask), (pair_hbm, pair),
    ]
    copies = [pltpu.make_async_copy(a, b, sems.at[i]) for i, (a, b) in enumerate(moves)]
    for copy in copies:
        copy.start()
    for copy in copies:
        copy.wait()
    weight_t = weight[...].T
    gate_t = gate[...].T
    wide = jnp.where((iota((T, C), 1) & (T - 1)) == iota((T, C), 0), 1.0, 0.0).astype(BF16)
    mask_rows = group_select(dot(mask[...].astype(F32).astype(BF16), wide))
    for s in range(8):
        x = jnp.concatenate([pair[8 * q + s].astype(F32) for q in range(4)], axis=0)
        normed = (normalize(x, 1) * gain[0:1, :] + bias[0:1, :]).astype(BF16)
        emit_operands(
            dot_nt(weight_t, normed), dot_nt(gate_t, normed), mask_rows[s : s + 1], scratch, s
        )
    lr[...] = scratch[...].reshape(C, 16, C).astype(BF16)


def first_side_kernel(
    pair, mask, in_gain, in_bias, weight, gate, out_gate, out_gain, out_bias, out_weight,
    zt, gt, weight_t, out_weight_t, columns, mask_rows, scratch,
):
    scratch[...] = pair[...].astype(F32).reshape(T * T, C)
    out_gate_t = out_gate[0].T
    for s in range(8):
        z = jnp.concatenate([scratch[pl.ds(8 * q + s, T, stride=T), :] for q in range(4)], axis=0)
        normed = (normalize(z, 1) * in_gain[0:1, :] + in_bias[0:1, :]).astype(BF16)
        zt[s] = z.T
        gt[s] = sigmoid(dot_nt(out_gate_t, normed))
    weight_t[: 2 * C] = weight[1].T
    weight_t[2 * C :] = gate[1].T
    out_weight_t[...] = out_weight[0].T
    columns[0] = as_column(out_gain[0:1, :])
    columns[1] = as_column(out_bias[0:1, :])
    columns[2] = as_column(in_gain[1:2, :])
    columns[3] = as_column(in_bias[1:2, :])
    columns[4] = as_column(out_gain[1:2, :])
    columns[5] = as_column(out_bias[1:2, :])
    four = jnp.concatenate([mask[...].astype(F32).astype(BF16)] * 4, axis=0)
    eye = jnp.where(iota((T, T), 1) == iota((T, T), 0), 1.0, 0.0).astype(BF16)
    mask_rows[...] = group_select(dot_nt(eye, four))


def middle_kernel(
    y, zt, gt, weight_t, out_weight_t, columns, mask_rows, lr, z_out, scratch, scratch_y
):
    scratch_y[...] = y[...].astype(F32).reshape(8 * C, C)
    for s in range(8):
        product = scratch_y[pl.ds(s, C, stride=8), :]
        product = (normalize(product, 0) * columns[0] + columns[1]).astype(BF16)
        z = (zt[s] + gt[s] * dot(out_weight_t[...], product)).astype(BF16)
        z_out[s] = z
        normed = (normalize(z.astype(F32), 0) * columns[2] + columns[3]).astype(BF16)
        emit_operands(
            dot(weight_t[: 2 * C], normed), dot(weight_t[2 * C :], normed),
            mask_rows[s : s + 1], scratch, s,
        )
    lr[...] = scratch[...].reshape(C, 16, C).astype(BF16)


def second_side_kernel(zt, in_gain, in_bias, out_gate, z_out, g_out):
    for s in range(8):
        z = zt[s].astype(F32).T
        normed = (normalize(z, 1) * in_gain[1:2, :] + in_bias[1:2, :]).astype(BF16)
        opened = sigmoid(dot(normed, out_gate[1]))
        for q in range(4):
            rows = pl.ds(8 * q + s, T, stride=T)
            z_out[rows, :] = z[q * T : (q + 1) * T]
            g_out[rows, :] = opened[q * T : (q + 1) * T]


def last_kernel(y, z_in, g_in, columns, out_weight, out, scratch_y):
    scratch_y[...] = y[...].astype(F32).reshape(8 * C, C)
    for s in range(8):
        product = scratch_y[pl.ds(s, C, stride=8), :]
        product = normalize(product, 0) * columns[4] + columns[5]
        update = dot(product.T.astype(BF16), out_weight[1])
        for q in range(4):
            rows = pl.ds((8 * q + s) * T, T)
            piece = z_in[rows, :] + g_in[rows, :] * update[q * T : (q + 1) * T]
            out[8 * q + s] = piece.astype(BF16)


def outgoing_kernel(core, own, other, out, left, right):
    swap = swap_groups()
    half = core[0]
    for part, src in enumerate((own, other)):
        for quad in range(2):
            y = jnp.concatenate(
                [src[:, 4 * quad + c].reshape(256, C) for c in range(4)], axis=1
            )
            z = dot(y, swap).reshape(16, 16, 4 * C)
            depth = pl.ds((2 * part + quad) * C, C)
            for q in range(4):
                left[:, q, :, depth] = z[:, :8, q * C : (q + 1) * C]
                right[:, q, :, depth] = z[:, 8:, q * C : (q + 1) * C]
    a = left[...].reshape(512, 512).astype(BF16)
    pairs = right.reshape(8, 2, 4, 8, 512)
    b = jnp.concatenate([pairs[:, half, q].reshape(64, 512) for q in range(4)], axis=0)
    product = dot_nt(b.astype(BF16), a).astype(BF16)
    for quad in range(4):
        y = jnp.concatenate(
            [product[64 * q : 64 * q + 64, quad * C : (quad + 1) * C] for q in range(4)], axis=1
        )
        z = dot(y, swap)
        for r in range(4):
            out[4 * quad + r] = z[:, r * C : (r + 1) * C].reshape(8, 8, C).astype(BF16)


def incoming_kernel(core, own, other, out, left, right):
    swap = swap_groups()
    half = core[0]
    for part, src in enumerate((own, other)):
        for quad in range(4):
            y = jnp.concatenate([src[4 * quad + r].reshape(C, C) for r in range(4)], axis=1)
            z = dot(y, swap).reshape(8, 16, 4 * C)
            depth = pl.ds(quad * C, C)
            for q in range(4):
                left[q, part, :, :, depth] = z[:, :8, q * C : (q + 1) * C]
                if part == 0:
                    right[:, q, :, depth] = z[:, 8:, q * C : (q + 1) * C]
    a = left[...].reshape(512, 512).astype(BF16)
    b = right[...].reshape(256, 512).astype(BF16)
    product = dot_nt(a, b).astype(BF16)
    for quad in range(2):
        y = jnp.concatenate(
            [product[C * q : C * q + C, quad * C : (quad + 1) * C] for q in range(4)], axis=1
        )
        z = dot(y, swap)
        for c in range(4):
            piece = z[:, c * C : (c + 1) * C].reshape(2, 8, 8, C).astype(BF16)
            out[:, half, 4 * quad + c] = piece[0]
            out[:, 1 - half, 4 * quad + c] = piece[1]


def call(kernel, out_shape, scratch, *args, smem=0, hbm=False):
    vmem = pl.BlockSpec(memory_space=pltpu.VMEM)
    scalars = pl.BlockSpec(memory_space=pltpu.SMEM)
    space = pl.BlockSpec(memory_space=pltpu.HBM) if hbm else vmem
    if hbm:
        args = [pltpu.with_memory_space_constraint(arg, pltpu.HBM) for arg in args]
    return pl.pallas_call(
        kernel,
        out_shape=out_shape,
        in_specs=[scalars] * smem + [space] * (len(args) - smem),
        out_specs=[vmem] * len(out_shape) if isinstance(out_shape, list) else vmem,
        scratch_shapes=scratch,
        compiler_params=pltpu.CompilerParams(vmem_limit_bytes=VMEM_LIMIT),
    )(*args)


def struct(shape, dtype):
    return jax.ShapeDtypeStruct(shape, dtype)


def exchange(values):
    return lax.all_to_all(values, CHIPS, 0, 0)


def other_core(values):
    return lax.ppermute(values, "core", [(0, 1), (1, 0)])


def on_device(
    pair, pair_mask, in_gain, in_bias, weight, gate, out_gate, out_gain, out_bias, out_weight
):
    core = lax.axis_index("core").astype(jnp.int32).reshape(1)
    operands = struct((C, 16, C), BF16)
    slabs = struct((8, C, C), F32)
    rows = struct((T * T, C), F32)
    sides = [pltpu.VMEM((16, 4, 8, 512), F32), pltpu.VMEM((16, 4, 8, 512), F32)]

    lr = call(
        first_kernel, operands,
        [
            pltpu.VMEM((T, T, C), BF16), pltpu.VMEM((T, T), jnp.int32),
            pltpu.VMEM((2, C), F32), pltpu.VMEM((2, C), F32),
            pltpu.VMEM((C, 2 * C), BF16), pltpu.VMEM((C, 2 * C), BF16),
            pltpu.VMEM((16 * C, C), F32), pltpu.SemaphoreType.DMA((6,)),
        ],
        pair, pair_mask, in_gain, in_bias, weight, gate, hbm=True,
    )
    own, side_pair = lax.optimization_barrier((exchange(lr), pair))
    other = other_core(own)
    zt, gt, weight_t, out_weight_t, columns, mask_rows = call(
        first_side_kernel,
        [
            slabs, slabs, struct((4 * C, C), BF16), struct((C, C), BF16),
            struct((6, C, C), F32), struct((8, C), F32),
        ],
        [pltpu.VMEM((T * T, C), F32)],
        side_pair, pair_mask, in_gain, in_bias, weight, gate, out_gate, out_gain, out_bias,
        out_weight,
    )
    other, zt = lax.optimization_barrier((other, zt))
    y = call(
        outgoing_kernel, struct((16, 8, 8, C), BF16), sides,
        core, own.reshape(16, 8, 16, C), other.reshape(16, 8, 16, C), smem=1,
    )
    y = exchange(y.reshape(C, 8, C))
    lr, zt = call(
        middle_kernel, [operands, struct((8, C, C), BF16)],
        [pltpu.VMEM((16 * C, C), F32), pltpu.VMEM((8 * C, C), F32)],
        y, zt, gt, weight_t, out_weight_t, columns, mask_rows,
    )
    own, zt = lax.optimization_barrier((exchange(lr), zt))
    other = other_core(own)
    z, g = call(second_side_kernel, [rows, rows], [], zt, in_gain, in_bias, out_gate)
    other, z = lax.optimization_barrier((other, z))
    y = call(
        incoming_kernel, struct((8, 2, 8, 8, C), BF16),
        [pltpu.VMEM((4, 2, 8, 8, 512), F32), pltpu.VMEM((8, 4, 8, 512), F32)],
        core, own.reshape(16, 8, 16, C), other.reshape(16, 8, 16, C), smem=1,
    )
    y = exchange(y.reshape(C, 8, C))
    return call(
        last_kernel, struct((T, T, C), BF16), [pltpu.VMEM((8 * C, C), F32)],
        y, z, g, columns, out_weight,
    )


def solution(mesh):
    chips = Mesh(mesh.devices.reshape((2,) * 8), AXES)
    tile = P(AXES[:4], AXES[4:])
    return jax.shard_map(
        on_device,
        mesh=chips,
        in_specs=(tile, tile) + (P(),) * 8,
        out_specs=tile,
        check_vma=False,
    )
```

```python
import jax
import jax.numpy as jnp
from jax import lax
from jax.experimental import pallas as pl
from jax.experimental.pallas import tpu as pltpu
from jax.sharding import Mesh
from jax.sharding import PartitionSpec as P

C = 128
T = 32
F32 = jnp.float32
BF16 = jnp.bfloat16
AXES = ("x1", "x0", "zh1", "zh0", "zl", "y1", "y0", "core")
FIRST = (2, 5, 2)


def away(place):
    x, z, y = place >> 5, (place >> 2) & 7, place & 3
    return (x - FIRST[0]) % 4, (z - FIRST[1]) % 8, (y - FIRST[2]) % 4


def hops(place):
    x, z, y = away(place)
    return min(x, 4 - x) + min(z, 8 - z) + min(y, 4 - y)


PLACES = sorted(range(C), key=lambda place: (hops(place) > 0, -hops(place), away(place)))
RANKS = {place: i for i, place in enumerate(PLACES)}
GROUPS = [[2 * place + core for place in PLACES] for core in range(2)]
VMEM_LIMIT = 32 * 1024 * 1024


def rank(row, pair_col):
    return RANKS[8 * row + pair_col]


def dot(a, b):
    return jnp.dot(a, b, preferred_element_type=F32)


def dot_nt(a, b):
    return lax.dot_general(a, b, (((1,), (1,)), ((), ())), preferred_element_type=F32)


def sigmoid(v):
    return 0.5 * jnp.tanh(0.5 * v) + 0.5


def normalize(values, axis):
    average = jnp.mean(values, axis=axis, keepdims=True)
    centered = values - average
    variance = jnp.mean(centered * centered, axis=axis, keepdims=True)
    return centered * lax.rsqrt(variance + 1e-05)


def iota(shape, dim):
    return lax.broadcasted_iota(jnp.int32, shape, dim)


def group_select(rows):
    group = iota((8, C), 1) // T
    out = rows[0:8]
    for q in range(1, 4):
        out = jnp.where(group == q, rows[8 * q : 8 * q + 8], out)
    return out


def as_column(vector):
    return jnp.broadcast_to(vector, (C, C)).T


def swap_groups():
    src = iota((4 * C, 4 * C), 0)
    dst = iota((4 * C, 4 * C), 1)
    back = (dst & (T - 1)) | (((dst >> 5) & 3) << 7) | ((dst >> 7) << 5)
    return jnp.where(src == back, 1.0, 0.0).astype(BF16)


def emit_operands(multiply, weight_t, gate_t, normed, mask_rows, scratch, s):
    masks = jnp.concatenate([mask_rows[s : s + 1], mask_rows[s + 1 : s + 2]], axis=1)
    operands = sigmoid(multiply(gate_t, normed)) * multiply(weight_t, normed) * masks
    for i in range(2):
        scratch[pl.ds(s + i, C, stride=16), :] = operands[:C, i * C : (i + 1) * C]
        scratch[pl.ds(8 + s + i, C, stride=16), :] = operands[C:, i * C : (i + 1) * C]


def first_kernel(
    pair_hbm, mask_hbm, gain_hbm, bias_hbm, weight_hbm, gate_hbm, lr,
    pair, mask, gain, bias, weight, gate, scratch, sems,
):
    moves = [
        (weight_hbm.at[0], weight), (gate_hbm.at[0], gate), (mask_hbm, mask),
        (gain_hbm, gain), (bias_hbm, bias), (pair_hbm, pair),
    ]
    copies = [pltpu.make_async_copy(a, b, sems.at[i]) for i, (a, b) in enumerate(moves)]
    for copy in copies:
        copy.start()
    wide = jnp.where((iota((T, C), 1) & (T - 1)) == iota((T, C), 0), 1.0, 0.0).astype(BF16)
    for copy in copies[:3]:
        copy.wait()
    weight_t = weight[...].T
    gate_t = gate[...].T
    mask_rows = group_select(dot(mask[...].astype(F32).astype(BF16), wide))
    for copy in copies[3:]:
        copy.wait()
    normed = []
    for s in range(0, 8, 2):
        tokens = [pair[8 * q + s + i].astype(F32) for i in range(2) for q in range(4)]
        x = normalize(jnp.concatenate(tokens, axis=0), 1)
        normed.append((x * gain[0:1, :] + bias[0:1, :]).astype(BF16))
    for s in range(0, 8, 2):
        emit_operands(dot_nt, weight_t, gate_t, normed[s // 2], mask_rows, scratch, s)
    lr[...] = scratch[...].reshape(C, 16, C).astype(BF16)


def first_side_kernel(
    pair, mask, in_gain, in_bias, weight, gate, out_gate, out_gain, out_bias, out_weight,
    zt, gt, weight_t, out_weight_t, columns, mask_rows, scratch,
):
    scratch[...] = pair[...].astype(F32).reshape(T * T, C)
    out_gate_t = out_gate[0].T
    for s in range(8):
        z = jnp.concatenate([scratch[pl.ds(8 * q + s, T, stride=T), :] for q in range(4)], axis=0)
        normed = (normalize(z, 1) * in_gain[0:1, :] + in_bias[0:1, :]).astype(BF16)
        zt[s] = z.T
        gt[s] = sigmoid(dot_nt(out_gate_t, normed))
    weight_t[: 2 * C] = weight[1].T
    weight_t[2 * C :] = gate[1].T
    out_weight_t[...] = out_weight[0].T
    columns[0] = as_column(out_gain[0:1, :])
    columns[1] = as_column(out_bias[0:1, :])
    columns[2] = as_column(in_gain[1:2, :])
    columns[3] = as_column(in_bias[1:2, :])
    columns[4] = as_column(out_gain[1:2, :])
    columns[5] = as_column(out_bias[1:2, :])
    four = jnp.concatenate([mask[...].astype(F32).astype(BF16)] * 4, axis=0)
    eye = jnp.where(iota((T, T), 1) == iota((T, T), 0), 1.0, 0.0).astype(BF16)
    mask_rows[...] = group_select(dot_nt(eye, four))


def middle_kernel(
    y, zt, gt, weight_t, out_weight_t, columns, mask_rows, lr, z_out, scratch, scratch_y
):
    scratch_y[...] = y[...].astype(F32).reshape(8 * C, C)
    twice = [jnp.concatenate([columns[i], columns[i]], axis=1) for i in range(4)]
    normed = []
    for s in range(0, 8, 2):
        slabs = [scratch_y[pl.ds(s + i, C, stride=8), :] for i in range(2)]
        product = normalize(jnp.concatenate(slabs, axis=1), 0)
        product = (product * twice[0] + twice[1]).astype(BF16)
        update = dot(out_weight_t[...], product)
        z = jnp.concatenate([zt[s], zt[s + 1]], axis=1)
        g = jnp.concatenate([gt[s], gt[s + 1]], axis=1)
        z = (z + g * update).astype(BF16)
        z_out[s] = z[:, :C]
        z_out[s + 1] = z[:, C:]
        normed.append((normalize(z.astype(F32), 0) * twice[2] + twice[3]).astype(BF16))
    for s in range(0, 8, 2):
        emit_operands(
            dot, weight_t[: 2 * C], weight_t[2 * C :], normed[s // 2], mask_rows[...], scratch, s
        )
    lr[...] = scratch[...].reshape(C, 16, C).astype(BF16)


def second_side_kernel(zt, in_gain, in_bias, out_gate, z_out, g_out):
    for s in range(8):
        z = zt[s].astype(F32).T
        normed = (normalize(z, 1) * in_gain[1:2, :] + in_bias[1:2, :]).astype(BF16)
        opened = sigmoid(dot(normed, out_gate[1]))
        for q in range(4):
            rows = pl.ds(8 * q + s, T, stride=T)
            z_out[rows, :] = z[q * T : (q + 1) * T]
            g_out[rows, :] = opened[q * T : (q + 1) * T]


def last_kernel(y, z_in, g_in, columns, out_weight, out, scratch_y):
    scratch_y[...] = y[...].astype(F32).reshape(8 * C, C)
    for s in range(8):
        product = scratch_y[pl.ds(s, C, stride=8), :]
        product = normalize(product, 0) * columns[4] + columns[5]
        update = dot(product.T.astype(BF16), out_weight[1])
        for q in range(4):
            rows = pl.ds((8 * q + s) * T, T)
            piece = z_in[rows, :] + g_in[rows, :] * update[q * T : (q + 1) * T]
            out[8 * q + s] = piece.astype(BF16)


def outgoing_kernel(core, own, other, out, left, right):
    swap = swap_groups()
    half = core[0]
    for part, src in enumerate((own, other)):
        for quad in range(2):
            y = jnp.concatenate(
                [
                    jnp.concatenate([src[rank(r, 4 * quad + c)] for r in range(16)], axis=0)
                    for c in range(4)
                ],
                axis=1,
            )
            z = dot(y, swap).reshape(16, 16, 4 * C)
            depth = pl.ds((2 * part + quad) * C, C)
            for q in range(4):
                left[:, q, :, depth] = z[:, :8, q * C : (q + 1) * C]
                right[:, q, :, depth] = z[:, 8:, q * C : (q + 1) * C]
    a = left[...].reshape(512, 512).astype(BF16)
    pairs = right.reshape(8, 2, 4, 8, 512)
    b = jnp.concatenate([pairs[:, half, q].reshape(64, 512) for q in range(4)], axis=0)
    product = dot_nt(b.astype(BF16), a).astype(BF16)
    for quad in range(4):
        y = jnp.concatenate(
            [product[64 * q : 64 * q + 64, quad * C : (quad + 1) * C] for q in range(4)], axis=1
        )
        z = dot(y, swap)
        for r in range(4):
            piece = z[:, r * C : (r + 1) * C].reshape(8, 8, C).astype(BF16)
            for c in range(8):
                out[rank(4 * quad + r, c)] = piece[c]


def incoming_kernel(core, own, other, out, left, right):
    swap = swap_groups()
    half = core[0]
    for part, src in enumerate((own, other)):
        for quad in range(4):
            y = jnp.concatenate(
                [
                    jnp.concatenate([src[rank(4 * quad + r, c)] for c in range(8)], axis=0)
                    for r in range(4)
                ],
                axis=1,
            )
            z = dot(y, swap).reshape(8, 16, 4 * C)
            depth = pl.ds(quad * C, C)
            for q in range(4):
                left[q, part, :, :, depth] = z[:, :8, q * C : (q + 1) * C]
                if part == 0:
                    right[:, q, :, depth] = z[:, 8:, q * C : (q + 1) * C]
    a = left[...].reshape(512, 512).astype(BF16)
    b = right[...].reshape(256, 512).astype(BF16)
    product = dot_nt(a, b).astype(BF16)
    for quad in range(2):
        y = jnp.concatenate(
            [product[C * q : C * q + C, quad * C : (quad + 1) * C] for q in range(4)], axis=1
        )
        z = dot(y, swap)
        for c in range(4):
            piece = z[:, c * C : (c + 1) * C].reshape(2, 8, 8, C).astype(BF16)
            for r in range(8):
                even, odd = rank(2 * r, 4 * quad + c), rank(2 * r + 1, 4 * quad + c)
                out[even + (odd - even) * half] = piece[0, r]
                out[odd - (odd - even) * half] = piece[1, r]


def call(kernel, out_shape, scratch, *args, smem=0, hbm=False):
    vmem = pl.BlockSpec(memory_space=pltpu.VMEM)
    scalars = pl.BlockSpec(memory_space=pltpu.SMEM)
    space = pl.BlockSpec(memory_space=pltpu.HBM) if hbm else vmem
    if hbm:
        args = [pltpu.with_memory_space_constraint(arg, pltpu.HBM) for arg in args]
    return pl.pallas_call(
        kernel,
        out_shape=out_shape,
        in_specs=[scalars] * smem + [space] * (len(args) - smem),
        out_specs=[vmem] * len(out_shape) if isinstance(out_shape, list) else vmem,
        scratch_shapes=scratch,
        compiler_params=pltpu.CompilerParams(vmem_limit_bytes=VMEM_LIMIT),
    )(*args)


def struct(shape, dtype):
    return jax.ShapeDtypeStruct(shape, dtype)


def exchange(values):
    return lax.all_to_all(values, AXES, 0, 0, axis_index_groups=GROUPS)


def other_core(values):
    return lax.ppermute(values, "core", [(0, 1), (1, 0)])


def on_device(
    pair, pair_mask, in_gain, in_bias, weight, gate, out_gate, out_gain, out_bias, out_weight
):
    core = lax.axis_index("core").astype(jnp.int32).reshape(1)
    operands = struct((C, 16, C), BF16)
    slabs = struct((8, C, C), F32)
    rows = struct((T * T, C), F32)
    sides = [pltpu.VMEM((16, 4, 8, 512), F32), pltpu.VMEM((16, 4, 8, 512), F32)]

    lr = call(
        first_kernel, operands,
        [
            pltpu.VMEM((T, T, C), BF16), pltpu.VMEM((T, T), jnp.int32),
            pltpu.VMEM((2, C), F32), pltpu.VMEM((2, C), F32),
            pltpu.VMEM((C, 2 * C), BF16), pltpu.VMEM((C, 2 * C), BF16),
            pltpu.VMEM((16 * C, C), F32), pltpu.SemaphoreType.DMA((6,)),
        ],
        pair, pair_mask, in_gain, in_bias, weight, gate, hbm=True,
    )
    own, side_pair = lax.optimization_barrier((exchange(lr), pair))
    other = other_core(own)
    zt, gt, weight_t, out_weight_t, columns, mask_rows = call(
        first_side_kernel,
        [
            slabs, slabs, struct((4 * C, C), BF16), struct((C, C), BF16),
            struct((6, C, C), F32), struct((8, C), F32),
        ],
        [pltpu.VMEM((T * T, C), F32)],
        side_pair, pair_mask, in_gain, in_bias, weight, gate, out_gate, out_gain, out_bias,
        out_weight,
    )
    other, zt = lax.optimization_barrier((other, zt))
    y = call(
        outgoing_kernel, struct((C, 8, C), BF16), sides,
        core, own, other, smem=1,
    )
    y = exchange(y)
    lr, zt = call(
        middle_kernel, [operands, struct((8, C, C), BF16)],
        [pltpu.VMEM((16 * C, C), F32), pltpu.VMEM((8 * C, C), F32)],
        y, zt, gt, weight_t, out_weight_t, columns, mask_rows,
    )
    own, zt = lax.optimization_barrier((exchange(lr), zt))
    other = other_core(own)
    z, g = call(second_side_kernel, [rows, rows], [], zt, in_gain, in_bias, out_gate)
    other, z = lax.optimization_barrier((other, z))
    y = call(
        incoming_kernel, struct((C, 8, C), BF16),
        [pltpu.VMEM((4, 2, 8, 8, 512), F32), pltpu.VMEM((8, 4, 8, 512), F32)],
        core, own, other, smem=1,
    )
    y = exchange(y)
    return call(
        last_kernel, struct((T, T, C), BF16), [pltpu.VMEM((8 * C, C), F32)],
        y, z, g, columns, out_weight,
    )


def solution(mesh):
    chips = Mesh(mesh.devices.reshape((2,) * 8), AXES)
    tile = P(AXES[:4], AXES[4:])
    return jax.shard_map(
        on_device,
        mesh=chips,
        in_specs=(tile, tile) + (P(),) * 8,
        out_specs=tile,
        check_vma=False,
    )
```

```python
import jax
import jax.numpy as jnp
from jax import lax
from jax.experimental import pallas as pl
from jax.experimental.pallas import tpu as pltpu
from jax.sharding import Mesh
from jax.sharding import PartitionSpec as P

C = 128
T = 32
F32 = jnp.float32
BF16 = jnp.bfloat16
AXES = ("x1", "x0", "zh1", "zh0", "zl", "y1", "y0", "core")
FIRST = (2, 5, 2)


def away(place):
    x, z, y = place >> 5, (place >> 2) & 7, place & 3
    return (x - FIRST[0]) % 4, (z - FIRST[1]) % 8, (y - FIRST[2]) % 4


def hops(place):
    x, z, y = away(place)
    return min(x, 4 - x) + min(z, 8 - z) + min(y, 4 - y)


def turn(place):
    x, z, y = away(place)
    return hops(place) > 0, -hops(place), -x, -z, -y


PLACES = sorted(range(C), key=turn)
RANKS = {place: i for i, place in enumerate(PLACES)}
GROUPS = [[2 * place + core for place in PLACES] for core in range(2)]
VMEM_LIMIT = 32 * 1024 * 1024


def rank(row, pair_col):
    return RANKS[8 * row + pair_col]


def dot(a, b):
    return jnp.dot(a, b, preferred_element_type=F32)


def dot_nt(a, b):
    return lax.dot_general(a, b, (((1,), (1,)), ((), ())), preferred_element_type=F32)


def sigmoid(v):
    return 0.5 * jnp.tanh(0.5 * v) + 0.5


def normalize(values, axis):
    average = jnp.mean(values, axis=axis, keepdims=True)
    centered = values - average
    variance = jnp.mean(centered * centered, axis=axis, keepdims=True)
    return centered * lax.rsqrt(variance + 1e-05)


def iota(shape, dim):
    return lax.broadcasted_iota(jnp.int32, shape, dim)


def group_select(rows):
    group = iota((8, C), 1) // T
    out = rows[0:8]
    for q in range(1, 4):
        out = jnp.where(group == q, rows[8 * q : 8 * q + 8], out)
    return out


def as_column(vector):
    return jnp.broadcast_to(vector, (C, C)).T


def swap_groups():
    src = iota((4 * C, 4 * C), 0)
    dst = iota((4 * C, 4 * C), 1)
    back = (dst & (T - 1)) | (((dst >> 5) & 3) << 7) | ((dst >> 7) << 5)
    return jnp.where(src == back, 1.0, 0.0).astype(BF16)


def emit_operands(multiply, weight_t, gate_t, normed, mask_rows, scratch, s):
    masks = jnp.concatenate([mask_rows[s : s + 1], mask_rows[s + 1 : s + 2]], axis=1)
    operands = sigmoid(multiply(gate_t, normed)) * multiply(weight_t, normed) * masks
    for i in range(2):
        scratch[pl.ds(s + i, C, stride=16), :] = operands[:C, i * C : (i + 1) * C]
        scratch[pl.ds(8 + s + i, C, stride=16), :] = operands[C:, i * C : (i + 1) * C]


def first_kernel(
    pair_hbm, mask_hbm, gain_hbm, bias_hbm, weight_hbm, gate_hbm, lr,
    pair, mask, gain, bias, weight, gate, scratch, sems,
):
    moves = [
        (weight_hbm.at[0], weight), (gate_hbm.at[0], gate), (mask_hbm, mask),
        (gain_hbm, gain), (bias_hbm, bias), (pair_hbm, pair),
    ]
    copies = [pltpu.make_async_copy(a, b, sems.at[i]) for i, (a, b) in enumerate(moves)]
    for copy in copies:
        copy.start()
    wide = jnp.where((iota((T, C), 1) & (T - 1)) == iota((T, C), 0), 1.0, 0.0).astype(BF16)
    for copy in copies[:3]:
        copy.wait()
    weight_t = weight[...].T
    gate_t = gate[...].T
    mask_rows = group_select(dot(mask[...].astype(F32).astype(BF16), wide))
    for copy in copies[3:]:
        copy.wait()
    normed = []
    for s in range(0, 8, 2):
        tokens = [pair[8 * q + s + i].astype(F32) for i in range(2) for q in range(4)]
        x = normalize(jnp.concatenate(tokens, axis=0), 1)
        normed.append((x * gain[0:1, :] + bias[0:1, :]).astype(BF16))
    for s in range(0, 8, 2):
        emit_operands(dot_nt, weight_t, gate_t, normed[s // 2], mask_rows, scratch, s)
    lr[...] = scratch[...].reshape(C, 16, C).astype(BF16)


def first_side_kernel(
    pair, mask, in_gain, in_bias, weight, gate, out_gate, out_gain, out_bias, out_weight,
    zt, gt, weight_t, out_weight_t, columns, mask_rows, scratch,
):
    scratch[...] = pair[...].astype(F32).reshape(T * T, C)
    out_gate_t = out_gate[0].T
    for s in range(8):
        z = jnp.concatenate([scratch[pl.ds(8 * q + s, T, stride=T), :] for q in range(4)], axis=0)
        normed = (normalize(z, 1) * in_gain[0:1, :] + in_bias[0:1, :]).astype(BF16)
        zt[s] = z.T
        gt[s] = sigmoid(dot_nt(out_gate_t, normed))
    weight_t[: 2 * C] = weight[1].T
    weight_t[2 * C :] = gate[1].T
    out_weight_t[...] = out_weight[0].T
    columns[0] = as_column(out_gain[0:1, :])
    columns[1] = as_column(out_bias[0:1, :])
    columns[2] = as_column(in_gain[1:2, :])
    columns[3] = as_column(in_bias[1:2, :])
    columns[4] = as_column(out_gain[1:2, :])
    columns[5] = as_column(out_bias[1:2, :])
    four = jnp.concatenate([mask[...].astype(F32).astype(BF16)] * 4, axis=0)
    eye = jnp.where(iota((T, T), 1) == iota((T, T), 0), 1.0, 0.0).astype(BF16)
    mask_rows[...] = group_select(dot_nt(eye, four))


def middle_kernel(
    y, zt, gt, weight_t, out_weight_t, columns, mask_rows, lr, z_out, scratch, scratch_y
):
    scratch_y[...] = y[...].astype(F32).reshape(8 * C, C)
    twice = [jnp.concatenate([columns[i], columns[i]], axis=1) for i in range(4)]
    normed = []
    for s in range(0, 8, 2):
        slabs = [scratch_y[pl.ds(s + i, C, stride=8), :] for i in range(2)]
        product = normalize(jnp.concatenate(slabs, axis=1), 0)
        product = (product * twice[0] + twice[1]).astype(BF16)
        update = dot(out_weight_t[...], product)
        z = jnp.concatenate([zt[s], zt[s + 1]], axis=1)
        g = jnp.concatenate([gt[s], gt[s + 1]], axis=1)
        z = (z + g * update).astype(BF16)
        z_out[s] = z[:, :C]
        z_out[s + 1] = z[:, C:]
        normed.append((normalize(z.astype(F32), 0) * twice[2] + twice[3]).astype(BF16))
    for s in range(0, 8, 2):
        emit_operands(
            dot, weight_t[: 2 * C], weight_t[2 * C :], normed[s // 2], mask_rows[...], scratch, s
        )
    lr[...] = scratch[...].reshape(C, 16, C).astype(BF16)


def second_side_kernel(zt, in_gain, in_bias, out_gate, z_out, g_out):
    for s in range(8):
        z = zt[s].astype(F32).T
        normed = (normalize(z, 1) * in_gain[1:2, :] + in_bias[1:2, :]).astype(BF16)
        opened = sigmoid(dot(normed, out_gate[1]))
        for q in range(4):
            rows = pl.ds(8 * q + s, T, stride=T)
            z_out[rows, :] = z[q * T : (q + 1) * T]
            g_out[rows, :] = opened[q * T : (q + 1) * T]


def last_kernel(y, z_in, g_in, columns, out_weight, out, scratch_y):
    scratch_y[...] = y[...].astype(F32).reshape(8 * C, C)
    for s in range(8):
        product = scratch_y[pl.ds(s, C, stride=8), :]
        product = normalize(product, 0) * columns[4] + columns[5]
        update = dot(product.T.astype(BF16), out_weight[1])
        for q in range(4):
            rows = pl.ds((8 * q + s) * T, T)
            piece = z_in[rows, :] + g_in[rows, :] * update[q * T : (q + 1) * T]
            out[8 * q + s] = piece.astype(BF16)


def regrouped(product):
    quads = [jnp.split(part, product.shape[1] // C, axis=1) for part in jnp.split(product, 4)]
    return jnp.concatenate([jnp.concatenate(parts, axis=1) for parts in zip(*quads)], axis=0)


def outgoing_kernel(core, own, other, out, left, right):
    swap = swap_groups()
    half = core[0]
    for part, src in enumerate((own, other)):
        for quad in range(2):
            y = jnp.concatenate(
                [
                    jnp.concatenate([src[rank(r, 4 * quad + c)] for r in range(16)], axis=0)
                    for c in range(4)
                ],
                axis=1,
            )
            z = dot(y, swap).reshape(16, 16, 4 * C)
            depth = pl.ds((2 * part + quad) * C, C)
            for q in range(4):
                left[:, q, :, depth] = z[:, :8, q * C : (q + 1) * C]
                right[:, q, :, depth] = z[:, 8:, q * C : (q + 1) * C]
    a = left[...].reshape(512, 512).astype(BF16)
    pairs = right.reshape(8, 2, 4, 8, 512)
    b = jnp.concatenate([pairs[:, half, q].reshape(64, 512) for q in range(4)], axis=0)
    product = dot_nt(b.astype(BF16), a).astype(BF16)
    z = dot(regrouped(product), swap)
    for r in range(16):
        quad, lanes = r // 4, slice(r % 4 * C, (r % 4 + 1) * C)
        piece = z[64 * quad : 64 * quad + 64, lanes].reshape(8, 8, C).astype(BF16)
        for c in range(8):
            out[rank(r, c)] = piece[c]


def incoming_kernel(core, own, other, out, left, right):
    swap = swap_groups()
    half = core[0]
    for part, src in enumerate((own, other)):
        for quad in range(4):
            y = jnp.concatenate(
                [
                    jnp.concatenate([src[rank(4 * quad + r, c)] for c in range(8)], axis=0)
                    for r in range(4)
                ],
                axis=1,
            )
            z = dot(y, swap).reshape(8, 16, 4 * C)
            depth = pl.ds(quad * C, C)
            for q in range(4):
                left[q, part, :, :, depth] = z[:, :8, q * C : (q + 1) * C]
                if part == 0:
                    right[:, q, :, depth] = z[:, 8:, q * C : (q + 1) * C]
    a = left[...].reshape(512, 512).astype(BF16)
    b = right[...].reshape(256, 512).astype(BF16)
    product = dot_nt(a, b).astype(BF16)
    z = dot(regrouped(product), swap)
    for c in range(8):
        quad, lanes = c // 4, slice(c % 4 * C, (c % 4 + 1) * C)
        piece = z[C * quad : C * quad + C, lanes].reshape(2, 8, 8, C).astype(BF16)
        for r in range(8):
            even, odd = rank(2 * r, c), rank(2 * r + 1, c)
            out[even + (odd - even) * half] = piece[0, r]
            out[odd - (odd - even) * half] = piece[1, r]


def call(kernel, out_shape, scratch, *args, smem=0, hbm=False):
    vmem = pl.BlockSpec(memory_space=pltpu.VMEM)
    scalars = pl.BlockSpec(memory_space=pltpu.SMEM)
    space = pl.BlockSpec(memory_space=pltpu.HBM) if hbm else vmem
    if hbm:
        args = [pltpu.with_memory_space_constraint(arg, pltpu.HBM) for arg in args]
    return pl.pallas_call(
        kernel,
        out_shape=out_shape,
        in_specs=[scalars] * smem + [space] * (len(args) - smem),
        out_specs=[vmem] * len(out_shape) if isinstance(out_shape, list) else vmem,
        scratch_shapes=scratch,
        compiler_params=pltpu.CompilerParams(vmem_limit_bytes=VMEM_LIMIT),
    )(*args)


def struct(shape, dtype):
    return jax.ShapeDtypeStruct(shape, dtype)


def exchange(values):
    return lax.all_to_all(values, AXES, 0, 0, axis_index_groups=GROUPS)


def other_core(values):
    return lax.ppermute(values, "core", [(0, 1), (1, 0)])


def on_device(
    pair, pair_mask, in_gain, in_bias, weight, gate, out_gate, out_gain, out_bias, out_weight
):
    core = lax.axis_index("core").astype(jnp.int32).reshape(1)
    operands = struct((C, 16, C), BF16)
    slabs = struct((8, C, C), F32)
    rows = struct((T * T, C), F32)
    sides = [pltpu.VMEM((16, 4, 8, 512), F32), pltpu.VMEM((16, 4, 8, 512), F32)]

    lr = call(
        first_kernel, operands,
        [
            pltpu.VMEM((T, T, C), BF16), pltpu.VMEM((T, T), jnp.int32),
            pltpu.VMEM((2, C), F32), pltpu.VMEM((2, C), F32),
            pltpu.VMEM((C, 2 * C), BF16), pltpu.VMEM((C, 2 * C), BF16),
            pltpu.VMEM((16 * C, C), F32), pltpu.SemaphoreType.DMA((6,)),
        ],
        pair, pair_mask, in_gain, in_bias, weight, gate, hbm=True,
    )
    own, side_pair = lax.optimization_barrier((exchange(lr), pair))
    other = other_core(own)
    zt, gt, weight_t, out_weight_t, columns, mask_rows = call(
        first_side_kernel,
        [
            slabs, slabs, struct((4 * C, C), BF16), struct((C, C), BF16),
            struct((6, C, C), F32), struct((8, C), F32),
        ],
        [pltpu.VMEM((T * T, C), F32)],
        side_pair, pair_mask, in_gain, in_bias, weight, gate, out_gate, out_gain, out_bias,
        out_weight,
    )
    other, zt = lax.optimization_barrier((other, zt))
    y = call(
        outgoing_kernel, struct((C, 8, C), BF16), sides,
        core, own, other, smem=1,
    )
    y = exchange(y)
    lr, zt = call(
        middle_kernel, [operands, struct((8, C, C), BF16)],
        [pltpu.VMEM((16 * C, C), F32), pltpu.VMEM((8 * C, C), F32)],
        y, zt, gt, weight_t, out_weight_t, columns, mask_rows,
    )
    own, zt = lax.optimization_barrier((exchange(lr), zt))
    other = other_core(own)
    z, g = call(second_side_kernel, [rows, rows], [], zt, in_gain, in_bias, out_gate)
    other, z = lax.optimization_barrier((other, z))
    y = call(
        incoming_kernel, struct((C, 8, C), BF16),
        [pltpu.VMEM((4, 2, 8, 8, 512), F32), pltpu.VMEM((8, 4, 8, 512), F32)],
        core, own, other, smem=1,
    )
    y = exchange(y)
    return call(
        last_kernel, struct((T, T, C), BF16), [pltpu.VMEM((8 * C, C), F32)],
        y, z, g, columns, out_weight,
    )


def solution(mesh):
    chips = Mesh(mesh.devices.reshape((2,) * 8), AXES)
    tile = P(AXES[:4], AXES[4:])
    return jax.shard_map(
        on_device,
        mesh=chips,
        in_specs=(tile, tile) + (P(),) * 8,
        out_specs=tile,
        check_vma=False,
    )
```

```python
import jax
import jax.numpy as jnp
from jax import lax
from jax.experimental import pallas as pl
from jax.experimental.pallas import tpu as pltpu
from jax.sharding import Mesh
from jax.sharding import PartitionSpec as P

C = 128
T = 32
F32 = jnp.float32
BF16 = jnp.bfloat16
AXES = ("x1", "x0", "zh1", "zh0", "zl", "y1", "y0", "core")
FIRST = (2, 5, 2)


def away(place):
    x, z, y = place >> 5, (place >> 2) & 7, place & 3
    return (x - FIRST[0]) % 4, (z - FIRST[1]) % 8, (y - FIRST[2]) % 4


def hops(place):
    x, z, y = away(place)
    return min(x, 4 - x) + min(z, 8 - z) + min(y, 4 - y)


def turn(place):
    x, z, y = away(place)
    return hops(place) > 0, -hops(place), -x, -z, -y


PLACES = sorted(range(C), key=turn)
RANKS = {place: i for i, place in enumerate(PLACES)}
GROUPS = [[2 * place + core for place in PLACES] for core in range(2)]
VMEM_LIMIT = 32 * 1024 * 1024


def rank(row, pair_col):
    return RANKS[8 * row + pair_col]


def dot(a, b):
    return jnp.dot(a, b, preferred_element_type=F32)


def dot_nt(a, b):
    return lax.dot_general(a, b, (((1,), (1,)), ((), ())), preferred_element_type=F32)


def sigmoid(v):
    return 0.5 * jnp.tanh(0.5 * v) + 0.5


def normalize(values, axis):
    average = jnp.mean(values, axis=axis, keepdims=True)
    centered = values - average
    variance = jnp.mean(centered * centered, axis=axis, keepdims=True)
    return centered * lax.rsqrt(variance + 1e-05)


def iota(shape, dim):
    return lax.broadcasted_iota(jnp.int32, shape, dim)


def group_select(rows):
    group = iota((8, C), 1) // T
    out = rows[0:8]
    for q in range(1, 4):
        out = jnp.where(group == q, rows[8 * q : 8 * q + 8], out)
    return out


def as_column(vector):
    return jnp.broadcast_to(vector, (C, C)).T


def swap_groups():
    src = iota((4 * C, 4 * C), 0)
    dst = iota((4 * C, 4 * C), 1)
    back = (dst & (T - 1)) | (((dst >> 5) & 3) << 7) | ((dst >> 7) << 5)
    return jnp.where(src == back, 1.0, 0.0).astype(BF16)


def emit_operands(multiply, weight_t, gate_t, normed, mask_rows, scratch, s):
    masks = jnp.concatenate([mask_rows[s : s + 1], mask_rows[s + 1 : s + 2]], axis=1)
    operands = sigmoid(multiply(gate_t, normed)) * multiply(weight_t, normed) * masks
    for i in range(2):
        scratch[pl.ds(s + i, C, stride=16), :] = operands[:C, i * C : (i + 1) * C]
        scratch[pl.ds(8 + s + i, C, stride=16), :] = operands[C:, i * C : (i + 1) * C]


def first_kernel(
    pair_hbm, mask_hbm, gain_hbm, bias_hbm, weight_hbm, gate_hbm,
    out_gate_hbm, out_gain_hbm, out_bias_hbm, out_weight_hbm,
    lr, pair, mask, gain, bias, weight, gate, out_gate, out_gain, out_bias, out_weight,
    scratch, sems,
):
    moves = [
        (weight_hbm.at[0], weight.at[0]), (gate_hbm.at[0], gate.at[0]), (mask_hbm, mask),
        (gain_hbm, gain), (bias_hbm, bias), (pair_hbm, pair),
        (weight_hbm.at[1], weight.at[1]), (gate_hbm.at[1], gate.at[1]),
        (out_gate_hbm, out_gate), (out_gain_hbm, out_gain),
        (out_bias_hbm, out_bias), (out_weight_hbm, out_weight),
    ]
    copies = [pltpu.make_async_copy(a, b, sems.at[i]) for i, (a, b) in enumerate(moves)]
    for copy in copies:
        copy.start()
    wide = jnp.where((iota((T, C), 1) & (T - 1)) == iota((T, C), 0), 1.0, 0.0).astype(BF16)
    for copy in copies[:3]:
        copy.wait()
    weight_t = weight[0].T
    gate_t = gate[0].T
    mask_rows = group_select(dot(mask[...].astype(F32).astype(BF16), wide))
    for copy in copies[3:6]:
        copy.wait()
    normed = []
    for s in range(0, 8, 2):
        tokens = [pair[8 * q + s + i].astype(F32) for i in range(2) for q in range(4)]
        x = normalize(jnp.concatenate(tokens, axis=0), 1)
        normed.append((x * gain[0:1, :] + bias[0:1, :]).astype(BF16))
    for s in range(0, 8, 2):
        emit_operands(dot_nt, weight_t, gate_t, normed[s // 2], mask_rows, scratch, s)
    lr[...] = scratch[...].reshape(C, 16, C).astype(BF16)
    for copy in copies[6:]:
        copy.wait()


def first_side_kernel(
    pair, mask, in_gain, in_bias, weight, gate, out_gate, out_gain, out_bias, out_weight,
    zt, gt, weight_t, out_weight_t, columns, mask_rows, scratch,
):
    scratch[...] = pair[...].astype(F32).reshape(T * T, C)
    out_gate_t = out_gate[0].T
    for s in range(8):
        z = jnp.concatenate([scratch[pl.ds(8 * q + s, T, stride=T), :] for q in range(4)], axis=0)
        normed = (normalize(z, 1) * in_gain[0:1, :] + in_bias[0:1, :]).astype(BF16)
        zt[s] = z.T
        gt[s] = sigmoid(dot_nt(out_gate_t, normed))
    weight_t[: 2 * C] = weight[1].T
    weight_t[2 * C :] = gate[1].T
    out_weight_t[...] = out_weight[0].T
    columns[0] = as_column(out_gain[0:1, :])
    columns[1] = as_column(out_bias[0:1, :])
    columns[2] = as_column(in_gain[1:2, :])
    columns[3] = as_column(in_bias[1:2, :])
    columns[4] = as_column(out_gain[1:2, :])
    columns[5] = as_column(out_bias[1:2, :])
    four = jnp.concatenate([mask[...].astype(F32).astype(BF16)] * 4, axis=0)
    eye = jnp.where(iota((T, T), 1) == iota((T, T), 0), 1.0, 0.0).astype(BF16)
    mask_rows[...] = group_select(dot_nt(eye, four))


def middle_kernel(
    y, zt, gt, weight_t, out_weight_t, columns, mask_rows, lr, z_out, scratch, scratch_y
):
    scratch_y[...] = y[...].astype(F32).reshape(8 * C, C)
    twice = [jnp.concatenate([columns[i], columns[i]], axis=1) for i in range(4)]
    normed = []
    for s in range(0, 8, 2):
        slabs = [scratch_y[pl.ds(s + i, C, stride=8), :] for i in range(2)]
        product = normalize(jnp.concatenate(slabs, axis=1), 0)
        product = (product * twice[0] + twice[1]).astype(BF16)
        update = dot(out_weight_t[...], product)
        z = jnp.concatenate([zt[s], zt[s + 1]], axis=1)
        g = jnp.concatenate([gt[s], gt[s + 1]], axis=1)
        z = (z + g * update).astype(BF16)
        z_out[s] = z[:, :C]
        z_out[s + 1] = z[:, C:]
        normed.append((normalize(z.astype(F32), 0) * twice[2] + twice[3]).astype(BF16))
    for s in range(0, 8, 2):
        emit_operands(
            dot, weight_t[: 2 * C], weight_t[2 * C :], normed[s // 2], mask_rows[...], scratch, s
        )
    lr[...] = scratch[...].reshape(C, 16, C).astype(BF16)


def second_side_kernel(zt, in_gain, in_bias, out_gate, z_out, g_out):
    for s in range(8):
        z = zt[s].astype(F32).T
        normed = (normalize(z, 1) * in_gain[1:2, :] + in_bias[1:2, :]).astype(BF16)
        opened = sigmoid(dot(normed, out_gate[1]))
        for q in range(4):
            rows = pl.ds(8 * q + s, T, stride=T)
            z_out[rows, :] = z[q * T : (q + 1) * T]
            g_out[rows, :] = opened[q * T : (q + 1) * T]


def last_kernel(y, z_in, g_in, columns, out_weight, out, scratch_y):
    scratch_y[...] = y[...].astype(F32).reshape(8 * C, C)
    for s in range(8):
        product = scratch_y[pl.ds(s, C, stride=8), :]
        product = normalize(product, 0) * columns[4] + columns[5]
        update = dot(product.T.astype(BF16), out_weight[1])
        for q in range(4):
            rows = pl.ds((8 * q + s) * T, T)
            piece = z_in[rows, :] + g_in[rows, :] * update[q * T : (q + 1) * T]
            out[8 * q + s] = piece.astype(BF16)


def regrouped(product):
    quads = [jnp.split(part, product.shape[1] // C, axis=1) for part in jnp.split(product, 4)]
    return jnp.concatenate([jnp.concatenate(parts, axis=1) for parts in zip(*quads)], axis=0)


def outgoing_sides(half, src, swap, left, right):
    for quad in range(2):
        y = jnp.concatenate(
            [
                jnp.concatenate([src[rank(r, 4 * quad + c)] for r in range(16)], axis=0)
                for c in range(4)
            ],
            axis=1,
        )
        z = dot(y, swap).reshape(16, 16, 4 * C)
        depth = pl.ds(quad * C, C)
        for q in range(4):
            left[:, q, :, depth] = z[:, :8, q * C : (q + 1) * C]
            right[:, q, :, depth] = z[:, 8:, q * C : (q + 1) * C]
    pairs = right.reshape(8, 2, 4, 8, 256)
    b = jnp.concatenate([pairs[:, half, q].reshape(64, 256) for q in range(4)], axis=0)
    return left[...].reshape(512, 256).astype(BF16), b.astype(BF16)


def outgoing_own_kernel(core, own, a_out, b_out, left, right):
    a_out[...], b_out[...] = outgoing_sides(core[0], own, swap_groups(), left, right)


def outgoing_kernel(core, other, a_own, b_own, out, left, right):
    swap = swap_groups()
    a, b = outgoing_sides(core[0], other, swap, left, right)
    product = (dot_nt(b_own[...], a_own[...]) + dot_nt(b, a)).astype(BF16)
    z = dot(regrouped(product), swap)
    for r in range(16):
        quad, lanes = r // 4, slice(r % 4 * C, (r % 4 + 1) * C)
        piece = z[64 * quad : 64 * quad + 64, lanes].reshape(8, 8, C).astype(BF16)
        for c in range(8):
            out[rank(r, c)] = piece[c]


def incoming_sides(src, swap, left, right):
    for quad in range(4):
        y = jnp.concatenate(
            [
                jnp.concatenate([src[rank(4 * quad + r, c)] for c in range(8)], axis=0)
                for r in range(4)
            ],
            axis=1,
        )
        z = dot(y, swap).reshape(8, 16, 4 * C)
        depth = pl.ds(quad * C, C)
        for q in range(4):
            left[q, :, :, depth] = z[:, :8, q * C : (q + 1) * C]
            if right is not None:
                right[:, q, :, depth] = z[:, 8:, q * C : (q + 1) * C]
    return left[...].reshape(256, 512).astype(BF16)


def incoming_own_kernel(own, a_out, b_out, left, right):
    a_out[...] = incoming_sides(own, swap_groups(), left, right)
    b_out[...] = right[...].reshape(256, 512).astype(BF16)


def incoming_kernel(core, other, a_own, b_own, out, left):
    swap = swap_groups()
    half = core[0]
    sides = (a_own[...], incoming_sides(other, swap, left, None))
    products = [dot_nt(a, b_own[...]).astype(BF16) for a in sides]
    z = dot(jnp.concatenate([regrouped(product) for product in products], axis=0), swap)
    for c in range(8):
        lanes = slice(c % 4 * C, (c % 4 + 1) * C)
        starts = [C * part + 64 * (c // 4) for part in range(2)]
        piece = [z[i : i + 64, lanes].reshape(8, 8, C).astype(BF16) for i in starts]
        for r in range(8):
            even, odd = rank(2 * r, c), rank(2 * r + 1, c)
            out[even + (odd - even) * half] = piece[0][r]
            out[odd - (odd - even) * half] = piece[1][r]


def call(kernel, out_shape, scratch, *args, smem=0, hbm=False):
    vmem = pl.BlockSpec(memory_space=pltpu.VMEM)
    scalars = pl.BlockSpec(memory_space=pltpu.SMEM)
    space = pl.BlockSpec(memory_space=pltpu.HBM) if hbm else vmem
    if hbm:
        args = [pltpu.with_memory_space_constraint(arg, pltpu.HBM) for arg in args]
    return pl.pallas_call(
        kernel,
        out_shape=out_shape,
        in_specs=[scalars] * smem + [space] * (len(args) - smem),
        out_specs=[vmem] * len(out_shape) if isinstance(out_shape, list) else vmem,
        scratch_shapes=scratch,
        compiler_params=pltpu.CompilerParams(vmem_limit_bytes=VMEM_LIMIT),
    )(*args)


def struct(shape, dtype):
    return jax.ShapeDtypeStruct(shape, dtype)


def exchange(values):
    return lax.all_to_all(values, AXES, 0, 0, axis_index_groups=GROUPS)


def other_core(values):
    return lax.ppermute(values, "core", [(0, 1), (1, 0)])


def on_device(
    pair, pair_mask, in_gain, in_bias, weight, gate, out_gate, out_gain, out_bias, out_weight
):
    core = lax.axis_index("core").astype(jnp.int32).reshape(1)
    operands = struct((C, 16, C), BF16)
    slabs = struct((8, C, C), F32)
    rows = struct((T * T, C), F32)
    sides = [pltpu.VMEM((16, 4, 8, 256), F32), pltpu.VMEM((16, 4, 8, 256), F32)]

    arguments = (
        pair, pair_mask, in_gain, in_bias, weight, gate, out_gate, out_gain, out_bias, out_weight
    )
    (
        lr, pair, pair_mask, in_gain, in_bias, weight, gate, out_gate, out_gain, out_bias, out_weight
    ) = call(
        first_kernel, [operands] + [struct(array.shape, array.dtype) for array in arguments],
        [pltpu.VMEM((16 * C, C), F32), pltpu.SemaphoreType.DMA((12,))],
        *arguments, hbm=True,
    )
    own = exchange(lr)
    other = other_core(own)
    a_own, b_own = call(
        outgoing_own_kernel, [struct((512, 256), BF16), struct((256, 256), BF16)], sides,
        core, own, smem=1,
    )
    zt, gt, weight_t, out_weight_t, columns, mask_rows = call(
        first_side_kernel,
        [
            slabs, slabs, struct((4 * C, C), BF16), struct((C, C), BF16),
            struct((6, C, C), F32), struct((8, C), F32),
        ],
        [pltpu.VMEM((T * T, C), F32)],
        pair, pair_mask, in_gain, in_bias, weight, gate, out_gate, out_gain, out_bias,
        out_weight,
    )
    other, zt, a_own = lax.optimization_barrier((other, zt, a_own))
    y = call(
        outgoing_kernel, struct((C, 8, C), BF16), sides, core, other, a_own, b_own, smem=1
    )
    y = exchange(y)
    lr, zt = call(
        middle_kernel, [operands, struct((8, C, C), BF16)],
        [pltpu.VMEM((16 * C, C), F32), pltpu.VMEM((8 * C, C), F32)],
        y, zt, gt, weight_t, out_weight_t, columns, mask_rows,
    )
    own, zt = lax.optimization_barrier((exchange(lr), zt))
    other = other_core(own)
    z, g = call(second_side_kernel, [rows, rows], [], zt, in_gain, in_bias, out_gate)
    left = pltpu.VMEM((4, 8, 8, 512), F32)
    a_own, b_own = call(
        incoming_own_kernel, [struct((256, 512), BF16), struct((256, 512), BF16)],
        [left, pltpu.VMEM((8, 4, 8, 512), F32)], own,
    )
    other, z, a_own = lax.optimization_barrier((other, z, a_own))
    y = call(
        incoming_kernel, struct((C, 8, C), BF16), [left], core, other, a_own, b_own, smem=1
    )
    y = exchange(y)
    return call(
        last_kernel, struct((T, T, C), BF16), [pltpu.VMEM((8 * C, C), F32)],
        y, z, g, columns, out_weight,
    )


def solution(mesh):
    chips = Mesh(mesh.devices.reshape((2,) * 8), AXES)
    tile = P(AXES[:4], AXES[4:])
    return jax.shard_map(
        on_device,
        mesh=chips,
        in_specs=(tile, tile) + (P(),) * 8,
        out_specs=tile,
        check_vma=False,
    )
```

```python
import jax
import jax.numpy as jnp
from jax import lax
from jax.experimental import pallas as pl
from jax.experimental.pallas import tpu as pltpu
from jax.sharding import Mesh
from jax.sharding import PartitionSpec as P

C = 128
T = 32
F32 = jnp.float32
BF16 = jnp.bfloat16
AXES = ("x1", "x0", "zh1", "zh0", "zl", "y1", "y0", "core")
FIRST = (2, 5, 2)


def away(place):
    x, z, y = place >> 5, (place >> 2) & 7, place & 3
    return (x - FIRST[0]) % 4, (z - FIRST[1]) % 8, (y - FIRST[2]) % 4


def hops(place):
    x, z, y = away(place)
    return min(x, 4 - x) + min(z, 8 - z) + min(y, 4 - y)


def turn(place):
    x, z, y = away(place)
    return hops(place) > 0, -hops(place), -x, -z, -y


PLACES = sorted(range(C), key=turn)
RANKS = {place: i for i, place in enumerate(PLACES)}
GROUPS = [[2 * place + core for place in PLACES] for core in range(2)]
VMEM_LIMIT = 32 * 1024 * 1024


def rank(row, pair_col):
    return RANKS[8 * row + pair_col]


def dot(a, b):
    return jnp.dot(a, b, preferred_element_type=F32)


def dot_nt(a, b):
    return lax.dot_general(a, b, (((1,), (1,)), ((), ())), preferred_element_type=F32)


def sigmoid(v):
    return 0.5 * jnp.tanh(0.5 * v) + 0.5


def normalize(values, axis):
    average = jnp.mean(values, axis=axis, keepdims=True)
    centered = values - average
    variance = jnp.mean(centered * centered, axis=axis, keepdims=True)
    return centered * lax.rsqrt(variance + 1e-05)


def iota(shape, dim):
    return lax.broadcasted_iota(jnp.int32, shape, dim)


def group_select(rows):
    group = iota((8, C), 1) // T
    out = rows[0:8]
    for q in range(1, 4):
        out = jnp.where(group == q, rows[8 * q : 8 * q + 8], out)
    return out


def as_column(vector):
    return jnp.broadcast_to(vector, (C, C)).T


def swap_groups():
    src = iota((4 * C, 4 * C), 0)
    dst = iota((4 * C, 4 * C), 1)
    back = (dst & (T - 1)) | (((dst >> 5) & 3) << 7) | ((dst >> 7) << 5)
    return jnp.where(src == back, 1.0, 0.0).astype(BF16)


def emit_operands(projected, gate, mask_rows, scratch, s):
    masks = jnp.concatenate([mask_rows[s : s + 1], mask_rows[s + 1 : s + 2]], axis=1)
    operands = sigmoid(gate) * projected * masks
    for i in range(2):
        scratch[pl.ds(s + i, C, stride=16), :] = operands[:C, i * C : (i + 1) * C]
        scratch[pl.ds(8 + s + i, C, stride=16), :] = operands[C:, i * C : (i + 1) * C]


def first_kernel(
    pair_hbm, mask_hbm, gain_hbm, bias_hbm, weight_hbm, gate_hbm,
    out_gate_hbm, out_gain_hbm, out_bias_hbm, out_weight_hbm,
    lr, pair, mask, gain, bias, weight, gate, out_gate, out_gain, out_bias, out_weight,
    scratch, sems,
):
    moves = [
        (weight_hbm.at[0], weight.at[0]), (gate_hbm.at[0], gate.at[0]), (mask_hbm, mask),
        (gain_hbm, gain), (bias_hbm, bias), (pair_hbm, pair),
        (weight_hbm.at[1], weight.at[1]), (gate_hbm.at[1], gate.at[1]),
        (out_gate_hbm, out_gate), (out_gain_hbm, out_gain),
        (out_bias_hbm, out_bias), (out_weight_hbm, out_weight),
    ]
    copies = [pltpu.make_async_copy(a, b, sems.at[i]) for i, (a, b) in enumerate(moves)]
    for copy in copies:
        copy.start()
    wide = jnp.where((iota((T, C), 1) & (T - 1)) == iota((T, C), 0), 1.0, 0.0).astype(BF16)
    for copy in copies[:3]:
        copy.wait()
    weight_t = weight[0].T
    gate_t = gate[0].T
    mask_rows = group_select(dot(mask[...].astype(F32).astype(BF16), wide))
    for copy in copies[3:6]:
        copy.wait()
    normed = []
    for s in range(0, 8, 2):
        tokens = [pair[8 * q + s + i].astype(F32) for i in range(2) for q in range(4)]
        x = normalize(jnp.concatenate(tokens, axis=0), 1)
        normed.append((x * gain[0:1, :] + bias[0:1, :]).astype(BF16))
    for s in range(0, 8, 2):
        tokens = normed[s // 2]
        emit_operands(dot_nt(weight_t, tokens), dot_nt(gate_t, tokens), mask_rows, scratch, s)
    lr[...] = scratch[...].reshape(C, 16, C).astype(BF16)
    for copy in copies[6:]:
        copy.wait()


def first_side_kernel(
    pair, mask, in_gain, in_bias, weight, gate, out_gate, out_gain, out_bias, out_weight,
    zt, gt, weight_t, out_weight_t, columns, mask_rows, scratch,
):
    scratch[...] = pair[...].astype(F32).reshape(T * T, C)
    out_gate_t = out_gate[0].T
    for s in range(8):
        z = jnp.concatenate([scratch[pl.ds(8 * q + s, T, stride=T), :] for q in range(4)], axis=0)
        normed = (normalize(z, 1) * in_gain[0:1, :] + in_bias[0:1, :]).astype(BF16)
        zt[s] = z.T
        gt[s] = sigmoid(dot_nt(out_gate_t, normed))
    weight_t[: 2 * C] = weight[1].T
    weight_t[2 * C :] = gate[1].T
    out_weight_t[...] = out_weight[0].T
    columns[0] = as_column(out_gain[0:1, :])
    columns[1] = as_column(out_bias[0:1, :])
    columns[2] = as_column(in_gain[1:2, :])
    columns[3] = as_column(in_bias[1:2, :])
    columns[4] = as_column(out_gain[1:2, :])
    columns[5] = as_column(out_bias[1:2, :])
    four = jnp.concatenate([mask[...].astype(F32).astype(BF16)] * 4, axis=0)
    eye = jnp.where(iota((T, T), 1) == iota((T, T), 0), 1.0, 0.0).astype(BF16)
    mask_rows[...] = group_select(dot_nt(eye, four))


def middle_kernel(
    y, zt, gt, weight_t, out_weight_t, columns, mask_rows, lr, z_out, scratch, scratch_y
):
    scratch_y[...] = y[...].astype(F32).reshape(8 * C, C)
    twice = [jnp.concatenate([columns[i], columns[i]], axis=1) for i in range(4)]
    normed = []
    for s in range(0, 8, 2):
        slabs = [scratch_y[pl.ds(s + i, C, stride=8), :] for i in range(2)]
        product = normalize(jnp.concatenate(slabs, axis=1), 0)
        product = (product * twice[0] + twice[1]).astype(BF16)
        update = dot(out_weight_t[...], product)
        z = jnp.concatenate([zt[s], zt[s + 1]], axis=1)
        g = jnp.concatenate([gt[s], gt[s + 1]], axis=1)
        z = (z + g * update).astype(BF16)
        z_out[s] = z[:, :C]
        z_out[s + 1] = z[:, C:]
        normed.append((normalize(z.astype(F32), 0) * twice[2] + twice[3]).astype(BF16))
    for s in range(0, 8, 2):
        both = dot(weight_t[...], normed[s // 2])
        emit_operands(both[: 2 * C], both[2 * C :], mask_rows[...], scratch, s)
    lr[...] = scratch[...].reshape(C, 16, C).astype(BF16)


def second_side_kernel(zt, in_gain, in_bias, out_gate, z_out, g_out):
    for s in range(8):
        z = zt[s].astype(F32).T
        normed = (normalize(z, 1) * in_gain[1:2, :] + in_bias[1:2, :]).astype(BF16)
        opened = sigmoid(dot(normed, out_gate[1]))
        for q in range(4):
            rows = pl.ds(8 * q + s, T, stride=T)
            z_out[rows, :] = z[q * T : (q + 1) * T]
            g_out[rows, :] = opened[q * T : (q + 1) * T]


def last_kernel(y, z_in, g_in, columns, out_weight, out, scratch_y):
    scratch_y[...] = y[...].astype(F32).reshape(8 * C, C)
    for s in range(8):
        product = scratch_y[pl.ds(s, C, stride=8), :]
        product = normalize(product, 0) * columns[4] + columns[5]
        update = dot(product.T.astype(BF16), out_weight[1])
        for q in range(4):
            rows = pl.ds((8 * q + s) * T, T)
            piece = z_in[rows, :] + g_in[rows, :] * update[q * T : (q + 1) * T]
            out[8 * q + s] = piece.astype(BF16)


def regrouped(product):
    quads = [jnp.split(part, product.shape[1] // C, axis=1) for part in jnp.split(product, 4)]
    return jnp.concatenate([jnp.concatenate(parts, axis=1) for parts in zip(*quads)], axis=0)


def outgoing_sides(half, src, swap, left, right):
    for quad in range(2):
        y = jnp.concatenate(
            [
                jnp.concatenate([src[rank(r, 4 * quad + c)] for r in range(16)], axis=0)
                for c in range(4)
            ],
            axis=1,
        )
        z = dot(y, swap).reshape(16, 16, 4 * C)
        depth = pl.ds(quad * C, C)
        for q in range(4):
            left[:, q, :, depth] = z[:, :8, q * C : (q + 1) * C]
            right[:, q, :, depth] = z[:, 8:, q * C : (q + 1) * C]
    pairs = right.reshape(8, 2, 4, 8, 256)
    b = jnp.concatenate([pairs[:, half, q].reshape(64, 256) for q in range(4)], axis=0)
    return left[...].reshape(512, 256).astype(BF16), b.astype(BF16)


def outgoing_own_kernel(core, own, a_out, b_out, left, right):
    a_out[...], b_out[...] = outgoing_sides(core[0], own, swap_groups(), left, right)


def outgoing_kernel(core, other, a_own, b_own, out, left, right):
    swap = swap_groups()
    a, b = outgoing_sides(core[0], other, swap, left, right)
    product = (dot_nt(b_own[...], a_own[...]) + dot_nt(b, a)).astype(BF16)
    z = dot(regrouped(product), swap)
    for r in range(16):
        quad, lanes = r // 4, slice(r % 4 * C, (r % 4 + 1) * C)
        piece = z[64 * quad : 64 * quad + 64, lanes].reshape(8, 8, C).astype(BF16)
        for c in range(8):
            out[rank(r, c)] = piece[c]


def incoming_sides(src, swap, left, right):
    for quad in range(4):
        y = jnp.concatenate(
            [
                jnp.concatenate([src[rank(4 * quad + r, c)] for c in range(8)], axis=0)
                for r in range(4)
            ],
            axis=1,
        )
        z = dot(y, swap).reshape(8, 16, 4 * C)
        depth = pl.ds(quad * C, C)
        for q in range(4):
            left[q, :, :, depth] = z[:, :8, q * C : (q + 1) * C]
            if right is not None:
                right[:, q, :, depth] = z[:, 8:, q * C : (q + 1) * C]
    return left[...].reshape(256, 512).astype(BF16)


def incoming_own_kernel(own, a_out, b_out, left, right):
    a_out[...] = incoming_sides(own, swap_groups(), left, right)
    b_out[...] = right[...].reshape(256, 512).astype(BF16)


def incoming_kernel(core, other, a_own, b_own, out, left):
    swap = swap_groups()
    half = core[0]
    sides = (a_own[...], incoming_sides(other, swap, left, None))
    products = [dot_nt(a, b_own[...]).astype(BF16) for a in sides]
    z = dot(jnp.concatenate([regrouped(product) for product in products], axis=0), swap)
    for c in range(8):
        lanes = slice(c % 4 * C, (c % 4 + 1) * C)
        starts = [C * part + 64 * (c // 4) for part in range(2)]
        piece = [z[i : i + 64, lanes].reshape(8, 8, C).astype(BF16) for i in starts]
        for r in range(8):
            even, odd = rank(2 * r, c), rank(2 * r + 1, c)
            out[even + (odd - even) * half] = piece[0][r]
            out[odd - (odd - even) * half] = piece[1][r]


def call(kernel, out_shape, scratch, *args, smem=0, hbm=False):
    vmem = pl.BlockSpec(memory_space=pltpu.VMEM)
    scalars = pl.BlockSpec(memory_space=pltpu.SMEM)
    space = pl.BlockSpec(memory_space=pltpu.HBM) if hbm else vmem
    if hbm:
        args = [pltpu.with_memory_space_constraint(arg, pltpu.HBM) for arg in args]
    return pl.pallas_call(
        kernel,
        out_shape=out_shape,
        in_specs=[scalars] * smem + [space] * (len(args) - smem),
        out_specs=[vmem] * len(out_shape) if isinstance(out_shape, list) else vmem,
        scratch_shapes=scratch,
        compiler_params=pltpu.CompilerParams(vmem_limit_bytes=VMEM_LIMIT),
    )(*args)


def struct(shape, dtype):
    return jax.ShapeDtypeStruct(shape, dtype)


def exchange(values):
    return lax.all_to_all(values, AXES, 0, 0, axis_index_groups=GROUPS)


def other_core(values):
    return lax.ppermute(values, "core", [(0, 1), (1, 0)])


def on_device(
    pair, pair_mask, in_gain, in_bias, weight, gate, out_gate, out_gain, out_bias, out_weight
):
    core = lax.axis_index("core").astype(jnp.int32).reshape(1)
    operands = struct((C, 16, C), BF16)
    slabs = struct((8, C, C), F32)
    rows = struct((T * T, C), F32)
    sides = [pltpu.VMEM((16, 4, 8, 256), F32), pltpu.VMEM((16, 4, 8, 256), F32)]

    arguments = (
        pair, pair_mask, in_gain, in_bias, weight, gate, out_gate, out_gain, out_bias, out_weight
    )
    (
        lr, pair, pair_mask, in_gain, in_bias, weight, gate, out_gate, out_gain, out_bias, out_weight
    ) = call(
        first_kernel, [operands] + [struct(array.shape, array.dtype) for array in arguments],
        [pltpu.VMEM((16 * C, C), F32), pltpu.SemaphoreType.DMA((12,))],
        *arguments, hbm=True,
    )
    own = exchange(lr)
    other = other_core(own)
    a_own, b_own = call(
        outgoing_own_kernel, [struct((512, 256), BF16), struct((256, 256), BF16)], sides,
        core, own, smem=1,
    )
    zt, gt, weight_t, out_weight_t, columns, mask_rows = call(
        first_side_kernel,
        [
            slabs, slabs, struct((4 * C, C), BF16), struct((C, C), BF16),
            struct((6, C, C), F32), struct((8, C), F32),
        ],
        [pltpu.VMEM((T * T, C), F32)],
        pair, pair_mask, in_gain, in_bias, weight, gate, out_gate, out_gain, out_bias,
        out_weight,
    )
    other, zt, a_own = lax.optimization_barrier((other, zt, a_own))
    y = call(
        outgoing_kernel, struct((C, 8, C), BF16), sides, core, other, a_own, b_own, smem=1
    )
    y = exchange(y)
    lr, zt = call(
        middle_kernel, [operands, struct((8, C, C), BF16)],
        [pltpu.VMEM((16 * C, C), F32), pltpu.VMEM((8 * C, C), F32)],
        y, zt, gt, weight_t, out_weight_t, columns, mask_rows,
    )
    own, zt = lax.optimization_barrier((exchange(lr), zt))
    other = other_core(own)
    z, g = call(second_side_kernel, [rows, rows], [], zt, in_gain, in_bias, out_gate)
    left = pltpu.VMEM((4, 8, 8, 512), F32)
    a_own, b_own = call(
        incoming_own_kernel, [struct((256, 512), BF16), struct((256, 512), BF16)],
        [left, pltpu.VMEM((8, 4, 8, 512), F32)], own,
    )
    other, z, a_own = lax.optimization_barrier((other, z, a_own))
    y = call(
        incoming_kernel, struct((C, 8, C), BF16), [left], core, other, a_own, b_own, smem=1
    )
    y = exchange(y)
    return call(
        last_kernel, struct((T, T, C), BF16), [pltpu.VMEM((8 * C, C), F32)],
        y, z, g, columns, out_weight,
    )


def solution(mesh):
    chips = Mesh(mesh.devices.reshape((2,) * 8), AXES)
    tile = P(AXES[:4], AXES[4:])
    return jax.shard_map(
        on_device,
        mesh=chips,
        in_specs=(tile, tile) + (P(),) * 8,
        out_specs=tile,
        check_vma=False,
    )
```

```python
import jax
import jax.numpy as jnp
from jax import lax
from jax.experimental import pallas as pl
from jax.experimental.pallas import tpu as pltpu
from jax.sharding import Mesh
from jax.sharding import PartitionSpec as P

C = 128
T = 32
F32 = jnp.float32
BF16 = jnp.bfloat16
AXES = ("x1", "x0", "zh1", "zh0", "zl", "y1", "y0", "core")
FIRST = (2, 5, 2)


def away(place):
    x, z, y = place >> 5, (place >> 2) & 7, place & 3
    return (x - FIRST[0]) % 4, (z - FIRST[1]) % 8, (y - FIRST[2]) % 4


def hops(place):
    x, z, y = away(place)
    return min(x, 4 - x) + min(z, 8 - z) + min(y, 4 - y)


def turn(place):
    x, z, y = away(place)
    return hops(place) > 0, -hops(place), -x, -z, -y


PLACES = sorted(range(C), key=turn)
RANKS = {place: i for i, place in enumerate(PLACES)}
GROUPS = [[2 * place + core for place in PLACES] for core in range(2)]
VMEM_LIMIT = 32 * 1024 * 1024


def rank(row, pair_col):
    return RANKS[8 * row + pair_col]


def dot(a, b):
    return jnp.dot(a, b, preferred_element_type=F32)


def dot_nt(a, b):
    return lax.dot_general(a, b, (((1,), (1,)), ((), ())), preferred_element_type=F32)


def sigmoid(v):
    return 0.5 * jnp.tanh(0.5 * v) + 0.5


def normalize(values, axis):
    average = jnp.mean(values, axis=axis, keepdims=True)
    centered = values - average
    variance = jnp.mean(centered * centered, axis=axis, keepdims=True)
    return centered * lax.rsqrt(variance + 1e-05)


def iota(shape, dim):
    return lax.broadcasted_iota(jnp.int32, shape, dim)


def group_select(rows):
    group = iota((8, C), 1) // T
    out = rows[0:8]
    for q in range(1, 4):
        out = jnp.where(group == q, rows[8 * q : 8 * q + 8], out)
    return out


def as_column(vector):
    return jnp.broadcast_to(vector, (C, C)).T


def swap_groups():
    src = iota((4 * C, 4 * C), 0)
    dst = iota((4 * C, 4 * C), 1)
    back = (dst & (T - 1)) | (((dst >> 5) & 3) << 7) | ((dst >> 7) << 5)
    return jnp.where(src == back, 1.0, 0.0).astype(BF16)


def emit_operands(multiply, weight_t, gate_t, normed, mask_rows, scratch, s):
    masks = jnp.concatenate([mask_rows[s : s + 1], mask_rows[s + 1 : s + 2]], axis=1)
    operands = sigmoid(multiply(gate_t, normed)) * multiply(weight_t, normed) * masks
    for i in range(2):
        scratch[pl.ds(s + i, C, stride=16), :] = operands[:C, i * C : (i + 1) * C]
        scratch[pl.ds(8 + s + i, C, stride=16), :] = operands[C:, i * C : (i + 1) * C]


def first_kernel(
    pair_hbm, mask_hbm, gain_hbm, bias_hbm, weight_hbm, gate_hbm,
    out_gate_hbm, out_gain_hbm, out_bias_hbm, out_weight_hbm,
    lr, pair, mask, gain, bias, weight, gate, out_gate, out_gain, out_bias, out_weight,
    scratch, sems,
):
    moves = [
        (weight_hbm.at[0], weight.at[0]), (gate_hbm.at[0], gate.at[0]), (mask_hbm, mask),
        (gain_hbm, gain), (bias_hbm, bias), (pair_hbm, pair),
        (weight_hbm.at[1], weight.at[1]), (gate_hbm.at[1], gate.at[1]),
        (out_gate_hbm, out_gate), (out_gain_hbm, out_gain),
        (out_bias_hbm, out_bias), (out_weight_hbm, out_weight),
    ]
    copies = [pltpu.make_async_copy(a, b, sems.at[i]) for i, (a, b) in enumerate(moves)]
    for copy in copies:
        copy.start()
    wide = jnp.where((iota((T, C), 1) & (T - 1)) == iota((T, C), 0), 1.0, 0.0).astype(BF16)
    for copy in copies[:3]:
        copy.wait()
    weight_t = weight[0].T
    gate_t = gate[0].T
    mask_rows = group_select(dot(mask[...].astype(F32).astype(BF16), wide))
    for copy in copies[3:6]:
        copy.wait()
    normed = []
    for s in range(0, 8, 2):
        tokens = [pair[8 * q + s + i].astype(F32) for i in range(2) for q in range(4)]
        x = normalize(jnp.concatenate(tokens, axis=0), 1)
        normed.append((x * gain[0:1, :] + bias[0:1, :]).astype(BF16))
    for s in range(0, 8, 2):
        emit_operands(dot_nt, weight_t, gate_t, normed[s // 2], mask_rows, scratch, s)
    lr[...] = scratch[...].reshape(C, 16, C).astype(BF16)
    for copy in copies[6:]:
        copy.wait()


def first_side_kernel(
    pair, mask, in_gain, in_bias, weight, gate, out_gate, out_gain, out_bias, out_weight,
    zt, gt, weight_t, out_weight_t, columns, mask_rows, scratch,
):
    scratch[...] = pair[...].astype(F32).reshape(T * T, C)
    out_gate_t = out_gate[0].T
    for s in range(8):
        z = jnp.concatenate([scratch[pl.ds(8 * q + s, T, stride=T), :] for q in range(4)], axis=0)
        normed = (normalize(z, 1) * in_gain[0:1, :] + in_bias[0:1, :]).astype(BF16)
        zt[s] = z.T
        gt[s] = sigmoid(dot_nt(out_gate_t, normed))
    weight_t[: 2 * C] = weight[1].T
    weight_t[2 * C :] = gate[1].T
    out_weight_t[...] = out_weight[0].T
    columns[0] = as_column(out_gain[0:1, :])
    columns[1] = as_column(out_bias[0:1, :])
    columns[2] = as_column(in_gain[1:2, :])
    columns[3] = as_column(in_bias[1:2, :])
    columns[4] = as_column(out_gain[1:2, :])
    columns[5] = as_column(out_bias[1:2, :])
    four = jnp.concatenate([mask[...].astype(F32).astype(BF16)] * 4, axis=0)
    eye = jnp.where(iota((T, T), 1) == iota((T, T), 0), 1.0, 0.0).astype(BF16)
    mask_rows[...] = group_select(dot_nt(eye, four))


def middle_kernel(
    y, zt, gt, weight_t, out_weight_t, columns, mask_rows, lr, z_out, scratch, scratch_y
):
    scratch_y[...] = y[...].astype(F32).reshape(8 * C, C)
    twice = [jnp.concatenate([columns[i], columns[i]], axis=1) for i in range(4)]
    normed = []
    for s in range(0, 8, 2):
        slabs = [scratch_y[pl.ds(s + i, C, stride=8), :] for i in range(2)]
        product = normalize(jnp.concatenate(slabs, axis=1), 0)
        product = (product * twice[0] + twice[1]).astype(BF16)
        update = dot(out_weight_t[...], product)
        z = jnp.concatenate([zt[s], zt[s + 1]], axis=1)
        g = jnp.concatenate([gt[s], gt[s + 1]], axis=1)
        z = (z + g * update).astype(BF16)
        z_out[s] = z[:, :C]
        z_out[s + 1] = z[:, C:]
        normed.append((normalize(z.astype(F32), 0) * twice[2] + twice[3]).astype(BF16))
    for s in range(0, 8, 2):
        emit_operands(
            dot, weight_t[: 2 * C], weight_t[2 * C :], normed[s // 2], mask_rows[...], scratch, s
        )
    lr[...] = scratch[...].reshape(C, 16, C).astype(BF16)


def second_side_kernel(zt, in_gain, in_bias, out_gate, z_out, g_out):
    for s in range(8):
        z = zt[s].astype(F32).T
        normed = (normalize(z, 1) * in_gain[1:2, :] + in_bias[1:2, :]).astype(BF16)
        opened = sigmoid(dot(normed, out_gate[1]))
        for q in range(4):
            rows = pl.ds(8 * q + s, T, stride=T)
            z_out[rows, :] = z[q * T : (q + 1) * T]
            g_out[rows, :] = opened[q * T : (q + 1) * T]


def last_kernel(y, z_in, g_in, columns, out_weight, out, scratch_y):
    scratch_y[...] = y[...].astype(F32).reshape(8 * C, C)
    for s in range(8):
        product = scratch_y[pl.ds(s, C, stride=8), :]
        product = normalize(product, 0) * columns[4] + columns[5]
        update = dot(product.T.astype(BF16), out_weight[1])
        for q in range(4):
            rows = pl.ds((8 * q + s) * T, T)
            piece = z_in[rows, :] + g_in[rows, :] * update[q * T : (q + 1) * T]
            out[8 * q + s] = piece.astype(BF16)


def regrouped(product):
    quads = [jnp.split(part, product.shape[1] // C, axis=1) for part in jnp.split(product, 4)]
    return jnp.concatenate([jnp.concatenate(parts, axis=1) for parts in zip(*quads)], axis=0)


def outgoing_sides(half, src, swap, left, right):
    for quad in range(2):
        y = jnp.concatenate(
            [
                jnp.concatenate([src[rank(r, 4 * quad + c)] for r in range(16)], axis=0)
                for c in range(4)
            ],
            axis=1,
        )
        z = dot(y, swap).reshape(16, 16, 4 * C)
        depth = pl.ds(quad * C, C)
        for q in range(4):
            left[:, q, :, depth] = z[:, :8, q * C : (q + 1) * C]
            right[:, q, :, depth] = z[:, 8:, q * C : (q + 1) * C]
    pairs = right.reshape(8, 2, 4, 8, 256)
    b = jnp.concatenate([pairs[:, half, q].reshape(64, 256) for q in range(4)], axis=0)
    return left[...].reshape(512, 256).astype(BF16), b.astype(BF16)


def outgoing_own_kernel(core, own, a_out, b_out, left, right):
    a_out[...], b_out[...] = outgoing_sides(core[0], own, swap_groups(), left, right)


def outgoing_kernel(core, other, a_own, b_own, out, left, right):
    swap = swap_groups()
    a, b = outgoing_sides(core[0], other, swap, left, right)
    product = (dot_nt(b_own[...], a_own[...]) + dot_nt(b, a)).astype(BF16)
    z = dot(regrouped(product), swap)
    for r in range(16):
        quad, lanes = r // 4, slice(r % 4 * C, (r % 4 + 1) * C)
        piece = z[64 * quad : 64 * quad + 64, lanes].reshape(8, 8, C).astype(BF16)
        for c in range(8):
            out[rank(r, c)] = piece[c]


def incoming_sides(src, swap, left, right):
    for quad in range(4):
        y = jnp.concatenate(
            [
                jnp.concatenate([src[rank(4 * quad + r, c)] for c in range(8)], axis=0)
                for r in range(4)
            ],
            axis=1,
        )
        z = dot(y, swap).reshape(8, 16, 4 * C)
        depth = pl.ds(quad * C, C)
        for q in range(4):
            left[q, :, :, depth] = z[:, :8, q * C : (q + 1) * C]
            right[:, q, :, depth] = z[:, 8:, q * C : (q + 1) * C]
    return left[...].reshape(256, 512).astype(BF16)


def incoming_own_kernel(own, a_out, b_out, left, right):
    a_out[...] = incoming_sides(own, swap_groups(), left, right)
    b_out[...] = right[...].reshape(256, 512).astype(BF16)


def incoming_kernel(core, a_other, a_own, b_own, out):
    swap = swap_groups()
    half = core[0]
    products = [dot_nt(a[...], b_own[...]).astype(BF16) for a in (a_own, a_other)]
    z = dot(jnp.concatenate([regrouped(product) for product in products], axis=0), swap)
    for c in range(8):
        lanes = slice(c % 4 * C, (c % 4 + 1) * C)
        starts = [C * part + 64 * (c // 4) for part in range(2)]
        piece = [z[i : i + 64, lanes].reshape(8, 8, C).astype(BF16) for i in starts]
        for r in range(8):
            even, odd = rank(2 * r, c), rank(2 * r + 1, c)
            out[even + (odd - even) * half] = piece[0][r]
            out[odd - (odd - even) * half] = piece[1][r]


def call(kernel, out_shape, scratch, *args, smem=0, hbm=False):
    vmem = pl.BlockSpec(memory_space=pltpu.VMEM)
    scalars = pl.BlockSpec(memory_space=pltpu.SMEM)
    space = pl.BlockSpec(memory_space=pltpu.HBM) if hbm else vmem
    if hbm:
        args = [pltpu.with_memory_space_constraint(arg, pltpu.HBM) for arg in args]
    return pl.pallas_call(
        kernel,
        out_shape=out_shape,
        in_specs=[scalars] * smem + [space] * (len(args) - smem),
        out_specs=[vmem] * len(out_shape) if isinstance(out_shape, list) else vmem,
        scratch_shapes=scratch,
        compiler_params=pltpu.CompilerParams(vmem_limit_bytes=VMEM_LIMIT),
    )(*args)


def struct(shape, dtype):
    return jax.ShapeDtypeStruct(shape, dtype)


def exchange(values):
    return lax.all_to_all(values, AXES, 0, 0, axis_index_groups=GROUPS)


def other_core(values):
    return lax.ppermute(values, "core", [(0, 1), (1, 0)])


def on_device(
    pair, pair_mask, in_gain, in_bias, weight, gate, out_gate, out_gain, out_bias, out_weight
):
    core = lax.axis_index("core").astype(jnp.int32).reshape(1)
    operands = struct((C, 16, C), BF16)
    slabs = struct((8, C, C), F32)
    rows = struct((T * T, C), F32)
    sides = [pltpu.VMEM((16, 4, 8, 256), F32), pltpu.VMEM((16, 4, 8, 256), F32)]

    arguments = (
        pair, pair_mask, in_gain, in_bias, weight, gate, out_gate, out_gain, out_bias, out_weight
    )
    (
        lr, pair, pair_mask, in_gain, in_bias, weight, gate, out_gate, out_gain, out_bias, out_weight
    ) = call(
        first_kernel, [operands] + [struct(array.shape, array.dtype) for array in arguments],
        [pltpu.VMEM((16 * C, C), F32), pltpu.SemaphoreType.DMA((12,))],
        *arguments, hbm=True,
    )
    own = exchange(lr)
    other = other_core(own)
    a_own, b_own = call(
        outgoing_own_kernel, [struct((512, 256), BF16), struct((256, 256), BF16)], sides,
        core, own, smem=1,
    )
    zt, gt, weight_t, out_weight_t, columns, mask_rows = call(
        first_side_kernel,
        [
            slabs, slabs, struct((4 * C, C), BF16), struct((C, C), BF16),
            struct((6, C, C), F32), struct((8, C), F32),
        ],
        [pltpu.VMEM((T * T, C), F32)],
        pair, pair_mask, in_gain, in_bias, weight, gate, out_gate, out_gain, out_bias,
        out_weight,
    )
    other, zt, a_own = lax.optimization_barrier((other, zt, a_own))
    y = call(
        outgoing_kernel, struct((C, 8, C), BF16), sides, core, other, a_own, b_own, smem=1
    )
    y = exchange(y)
    lr, zt = call(
        middle_kernel, [operands, struct((8, C, C), BF16)],
        [pltpu.VMEM((16 * C, C), F32), pltpu.VMEM((8 * C, C), F32)],
        y, zt, gt, weight_t, out_weight_t, columns, mask_rows,
    )
    a_own, b_own = call(
        incoming_own_kernel, [struct((256, 512), BF16), struct((256, 512), BF16)],
        [pltpu.VMEM((4, 8, 8, 512), F32), pltpu.VMEM((8, 4, 8, 512), F32)], exchange(lr),
    )
    a_own, zt = lax.optimization_barrier((a_own, zt))
    a_other = other_core(a_own)
    z, g = call(second_side_kernel, [rows, rows], [], zt, in_gain, in_bias, out_gate)
    a_other, z = lax.optimization_barrier((a_other, z))
    y = call(
        incoming_kernel, struct((C, 8, C), BF16), [], core, a_other, a_own, b_own, smem=1
    )
    y = exchange(y)
    return call(
        last_kernel, struct((T, T, C), BF16), [pltpu.VMEM((8 * C, C), F32)],
        y, z, g, columns, out_weight,
    )


def solution(mesh):
    chips = Mesh(mesh.devices.reshape((2,) * 8), AXES)
    tile = P(AXES[:4], AXES[4:])
    return jax.shard_map(
        on_device,
        mesh=chips,
        in_specs=(tile, tile) + (P(),) * 8,
        out_specs=tile,
        check_vma=False,
    )
```
